32 devices in a mesh: dp: 16 (over z, y, core), mp: 2 (over x).
Axes of the slice: x: 2, y: 2, z: 4, core: 2. Of those that a mesh axis runs over, the one named last changes fastest.
Arguments:
- layer_input: bfloat16 [49152, 1024], P('dp'), may hold values from -11 to 11
- out_cotangent: bfloat16 [49152, 1024], P(('dp', 'mp')), may hold values from -6 to 6
- segment_ids: int32 [16, 3072], P('dp'), may hold values from 0 to 2, as said below
- qkv_weight: float32 [3, 1024, 1024], P(None, 'dp', 'mp'), may hold values from -0.1875 to 0.1875
- out_weight: float32 [1024, 1024], P('dp', 'mp'), may hold values from -6 to 6
- up_weight: float32 [1024, 4096], P('dp', 'mp'), may hold values from -0.1875 to 0.1875
- down_weight: float32 [1024, 4096], P('dp', 'mp'), may hold values from -0.09375 to 0.09375
- norm_gains: float32 [2, 1024], replicated, may hold values from 0.5 to 1.5
- bias_rows: float32 [6, 1024], replicated, may hold values from -4 to 4
- up_bias: float32 [4096], replicated, may hold values from -4 to 4
- qkv_moments: float32 [2, 3, 1024, 1024], P(None, None, 'dp', 'mp'), may hold values from -2 to 2, as said below
- out_moments: float32 [2, 1024, 1024], P(None, 'dp', 'mp'), may hold values from -2 to 2, as said below
- up_moments: float32 [2, 1024, 4096], P(None, 'dp', 'mp'), may hold values from -2 to 2, as said below
- down_moments: float32 [2, 1024, 4096], P(None, 'dp', 'mp'), may hold values from -2 to 2, as said below
- gain_moments: float32 [2, 2, 1024], replicated, may hold values from -2 to 2, as said below
- bias_moments: float32 [2, 6, 1024], replicated, may hold values from -2 to 2, as said below
- up_bias_moments: float32 [2, 4096], replicated, may hold values from -2 to 2, as said below
Outputs:
- layer_output: bfloat16 [49152, 1024], P(('dp', 'mp'))
- input_grad: float32 [49152, 1024], P(('dp', 'mp'))
- new_qkv: float32 [3, 1024, 1024], P(None, 'dp', 'mp')
- new_out: float32 [1024, 1024], P('dp', 'mp')
- new_up: float32 [1024, 4096], P('dp', 'mp')
- new_down: float32 [1024, 4096], P('dp', 'mp')
- new_gains: float32 [2, 1024], replicated
- new_biases: float32 [6, 1024], replicated
- new_up_bias: float32 [4096], replicated
- next_qkv_moments: float32 [2, 3, 1024, 1024], P(None, None, 'dp', 'mp')
- next_out_moments: float32 [2, 1024, 1024], P(None, 'dp', 'mp')
- next_up_moments: float32 [2, 1024, 4096], P(None, 'dp', 'mp')
- next_down_moments: float32 [2, 1024, 4096], P(None, 'dp', 'mp')
- next_gain_moments: float32 [2, 2, 1024], replicated
- next_bias_moments: float32 [2, 6, 1024], replicated
- next_up_bias_moments: float32 [2, 4096], replicated
The draws below stay inside these ranges and needn't reach their ends.
Inputs may be any that keep to these rules, and one draw needn't show every extreme that they name: `segment_ids`: ids never fall along a sequence and start at 0; a sequence holds at most three documents, one of which begins within its first 384 tokens and ends within its last 384. `qkv_moments`: index 0 of the first dimension holds first moments, index 1 positive second moments. `out_moments`: index 0 of the first dimension holds first moments, index 1 positive second moments. `up_moments`: index 0 of the first dimension holds first moments, index 1 positive second moments. `down_moments`: index 0 of the first dimension holds first moments, index 1 positive second moments. `gain_moments`: index 0 of the first dimension holds first moments, index 1 positive second moments. `bias_moments`: index 0 of the first dimension holds first moments, index 1 positive second moments. `up_bias_moments`: index 0 of the first dimension holds first moments, index 1 positive second moments.
All inputs are finite; a program needn't handle non-finite values.
Results may differ from the reference program's by a relative error of at most 0.019.
The reference program's roundings to bfloat16 on the way count: a program that leaves them out, or rounds other values in their place, can miss the bound.
Values may be sent and summed in bfloat16 or wider, within the bound.
No kernel may reach another device: no remote copies, remote signals or barrier semaphores. Data moves between devices by JAX's collectives and lax.ppermute only.
A program may use at most 384 MiB of HBM per device.

```python
import math
import jax
import jax.numpy as jnp
from jax import lax

D = 1024
HEADS = 16
HEAD_DIM = 64
FF = 4096
SEQ_LEN = 3072
ADAM_STEP = 5
SEQS = 16
TOKENS = 49152


def draw_layer_input(key, part):
    position = jnp.arange(TOKENS, dtype=jnp.float32) / max(TOKENS - 1, 1)
    scale_col = (1.0 + 0.75 * position)[:, None]
    base = jax.random.truncated_normal(key, -6.0, 6.0, (TOKENS, D), jnp.float32)
    return (base * scale_col).astype(jnp.bfloat16)


def draw_segment_ids(key, part):
    own_key = jax.random.fold_in(key, 71)
    start_key = jax.random.fold_in(own_key, 1)
    end_key = jax.random.fold_in(own_key, 2)
    margin = SEQ_LEN // 8
    starts = jax.random.randint(start_key, (SEQS, 1), 0, margin + 1)
    ends = jax.random.randint(end_key, (SEQS, 1), SEQ_LEN - margin, SEQ_LEN + 1)
    position = jnp.arange(SEQ_LEN, dtype=jnp.int32)[None, :]
    first_part = jnp.where((position >= starts) & (starts > 0), 1, 0)
    last_part = jnp.where(position >= ends, 1, 0)
    return (first_part + last_part).astype(jnp.int32)


def moment_pair(key, shape, label, size_factor):
    own_key = jax.random.fold_in(key, label)
    first_key = jax.random.fold_in(own_key, 11)
    second_key = jax.random.fold_in(own_key, 23)
    first_moment = 0.3 * size_factor * jax.random.truncated_normal(first_key, -6.0, 6.0, shape, jnp.float32)
    second_moment = size_factor * size_factor * jnp.exp(jax.random.uniform(second_key, shape, jnp.float32, math.log(0.01), 0.0))
    return jnp.stack([first_moment, second_moment])


def draw_qkv_moments(key, part):
    return moment_pair(key, (3, D, D), 101, 1.0)


def draw_out_moments(key, part):
    return moment_pair(key, (D, D), 102, math.sqrt(min(1.0, 64.0 / SEQ_LEN)))


def draw_up_moments(key, part):
    return moment_pair(key, (D, FF), 103, 1.0)


def draw_down_moments(key, part):
    return moment_pair(key, (D, FF), 104, 1.0)


def draw_gain_moments(key, part):
    return moment_pair(key, (2, D), 105, 1.0)


def draw_bias_moments(key, part):
    return moment_pair(key, (6, D), 106, 1.0)


def draw_up_bias_moments(key, part):
    return moment_pair(key, (FF,), 107, 1.0)


def shard_levels(rng, shape, shards, least, high):
    gain, own = 1.0, jax.random.fold_in(rng, 6)
    for dim, shards_of in shards:
        heights = jnp.exp(jax.random.uniform(jax.random.fold_in(own, dim), (shards_of,), jnp.float32, least / len(shards), high / len(shards)))
        gain = gain * jnp.repeat(heights, shape[dim] // shards_of).reshape([-1 if axis == dim else 1 for axis in range(len(shape))])
    return gain


def centred(stream_key, shape, scale, limit, cuts=(), kind=jnp.bfloat16):
    entries = jax.random.normal(stream_key, shape, jnp.float32) * scale
    if len(cuts) > 0:
        entries = shard_levels(stream_key, shape, cuts, -0.22, 0.18) * entries
    return jnp.clip(entries, min=-limit, max=limit).astype(kind)


def setup_inputs(seed: int = 0) -> dict:
    seeds = jax.random.split(jax.random.key(seed), 18)
    layer_input = draw_layer_input(jax.random.fold_in(seeds[17], 71), 0)
    out_cotangent = centred(seeds[1], (TOKENS, D), 1.0, 6.0, ((0, 32),))
    segment_ids = draw_segment_ids(jax.random.fold_in(seeds[17], 71), 0)
    qkv_weight = centred(seeds[3], (3, D, D), D ** -0.5, 0.1875, ((1, 16), (2, 2)), jnp.float32)
    out_weight = centred(seeds[4], (D, D), (max(1, D * 4 // SEQ_LEN)) ** -0.5, 6.0, ((0, 16), (1, 2)), jnp.float32)
    up_weight = centred(seeds[5], (D, FF), D ** -0.5, 0.1875, ((0, 16), (1, 2)), jnp.float32)
    down_weight = centred(seeds[6], (D, FF), FF ** -0.5, 0.09375, ((0, 16), (1, 2)), jnp.float32)
    norm_gains = jnp.clip(1.0 + 0.1 * jax.random.normal(seeds[7], (2, D), jnp.float32), 0.5, 1.5)
    bias_rows = centred(seeds[8], (6, D), 0.3, 4.0, (), jnp.float32)
    up_bias = centred(seeds[9], (FF,), 0.3, 4.0, (), jnp.float32)
    qkv_moments = draw_qkv_moments(jax.random.fold_in(seeds[17], 71), 0)
    out_moments = draw_out_moments(jax.random.fold_in(seeds[17], 71), 0)
    up_moments = draw_up_moments(jax.random.fold_in(seeds[17], 71), 0)
    down_moments = draw_down_moments(jax.random.fold_in(seeds[17], 71), 0)
    gain_moments = draw_gain_moments(jax.random.fold_in(seeds[17], 71), 0)
    bias_moments = draw_bias_moments(jax.random.fold_in(seeds[17], 71), 0)
    up_bias_moments = draw_up_bias_moments(jax.random.fold_in(seeds[17], 71), 0)
    return {"layer_input": layer_input, "out_cotangent": out_cotangent, "segment_ids": segment_ids, "qkv_weight": qkv_weight, "out_weight": out_weight, "up_weight": up_weight, "down_weight": down_weight, "norm_gains": norm_gains, "bias_rows": bias_rows, "up_bias": up_bias, "qkv_moments": qkv_moments, "out_moments": out_moments, "up_moments": up_moments, "down_moments": down_moments, "gain_moments": gain_moments, "bias_moments": bias_moments, "up_bias_moments": up_bias_moments}


@jax.custom_vjp
def low(v):
    return lax.optimization_barrier(v.astype(jnp.bfloat16)).astype(jnp.float32)

@jax.custom_vjp
def low_back(v):
    return v

def low_keep(v):
    return (low(v), None)

def low_pass(kept, grad):
    return (grad,)

def back_keep(v):
    return (v, None)

def back_low(kept, grad):
    return (low(grad),)
low.defvjp(low_keep, low_pass)
low_back.defvjp(back_keep, back_low)
highest = lax.Precision.HIGHEST
very_low = -1e+30
clip_tau = 5.0
learn_rate = 0.25
weight_decay = 0.1
moment_beta = 0.5
adam_epsilon = 1e-08

def norm_rows(values, gain_row, shift_row):
    center = values - lax.optimization_barrier(jnp.mean(values, axis=-1, keepdims=True))
    spread = lax.optimization_barrier(jnp.mean(center * center, axis=-1, keepdims=True))
    return center * lax.rsqrt(spread + 1e-05) * gain_row + shift_row

def attend_block(query_block, key_heads, value_heads, query_ids, key_ids):
    scores = low_back(jnp.einsum('qhd,khd->hqk', query_block, key_heads, precision=highest) * HEAD_DIM ** (-0.5))
    allowed = (query_ids[:, None] == key_ids[None, :])[None]
    masked = jnp.where(allowed, scores, very_low)
    probs = jax.nn.softmax(masked, axis=-1)
    output = jnp.einsum('hqk,khd->qhd', low(probs), value_heads, precision=highest)
    return (output, lax.optimization_barrier(jnp.max(masked, axis=(1, 2))))

def sequence_attention(queries, keys_all, values_all, seg_row):
    length = queries.shape[0]
    block_rows = min(512, length)
    block_total = length // block_rows
    query_blocks = queries.reshape(block_total, block_rows, HEADS, HEAD_DIM)
    id_blocks = seg_row.reshape(block_total, block_rows)
    key_heads = keys_all.reshape(length, HEADS, HEAD_DIM)
    value_heads = values_all.reshape(length, HEADS, HEAD_DIM)

    def one_block(block_pair):
        return attend_block(block_pair[0], key_heads, value_heads, block_pair[1], seg_row)
    outputs, maxima = lax.map(jax.checkpoint(one_block), (query_blocks, id_blocks))
    return (outputs.reshape(length, D), lax.optimization_barrier(jnp.max(maxima, axis=0)))

def layer(weight_set, inputs, seg_row):
    qkv_weight, out_weight, up_weight, down_weight, norm_gains, bias_rows, up_bias = weight_set
    qkv_low = low(qkv_weight)
    out_low = low(out_weight)
    up_low = low(up_weight)
    down_low = low(down_weight)
    projected = jnp.einsum('td,cde->cte', inputs, qkv_low, precision=highest)
    queries = low(low_back(projected[0]) + bias_rows[0])
    keys_all = low(low_back(projected[1]))
    values_all = low(low_back(projected[2]) + bias_rows[1])
    attended, maxima = sequence_attention(queries, keys_all, values_all, seg_row)
    attended = low(low_back(attended))
    branch = low_back(jnp.dot(attended, out_low.T, precision=highest))
    summed = inputs + branch + bias_rows[2]
    normed = norm_rows(summed, norm_gains[0], bias_rows[4])
    pre_act = low_back(jnp.dot(low(normed), up_low, precision=highest)) + up_bias
    hidden = low(jax.nn.gelu(pre_act, approximate=False))
    ffn_out = low_back(jnp.dot(hidden, down_low.T, precision=highest))
    total = normed + ffn_out + bias_rows[3]
    return (norm_rows(total, norm_gains[1], bias_rows[5]), maxima)

def adam_update(param, moments, grad, step_value):
    first_moment = moment_beta * moments[0] + (1.0 - moment_beta) * grad
    second_moment = moment_beta * moments[1] + (1.0 - moment_beta) * grad * grad
    correct = 1.0 - jnp.power(moment_beta, step_value)
    update = first_moment / correct / (jnp.sqrt(second_moment / correct) + adam_epsilon)
    return (param - learn_rate * (update + weight_decay * param), jnp.stack([first_moment, second_moment]))

def reference(layer_input, out_cotangent, segment_ids, qkv_weight, out_weight, up_weight, down_weight, norm_gains, bias_rows, up_bias, qkv_moments, out_moments, up_moments, down_moments, gain_moments, bias_moments, up_bias_moments):
    weight_set = (qkv_weight, out_weight, up_weight, down_weight, norm_gains, bias_rows, up_bias)
    inputs = layer_input.astype(jnp.float32).reshape(SEQS, SEQ_LEN, D)
    cotangents = out_cotangent.astype(jnp.float32).reshape(SEQS, SEQ_LEN, D)
    zero_grads = jax.tree.map(jnp.zeros_like, weight_set)

    def one_sequence(running, items):
        grads_sum, top_scores = running
        seq_input, seq_cotangent, seq_ids = items

        def inner(weights_now, input_now):
            return layer(weights_now, input_now, seq_ids)
        outputs, pullback, maxima = jax.vjp(inner, weight_set, seq_input, has_aux=True)
        weight_grads, input_grads = pullback(seq_cotangent)
        grads_sum = jax.tree.map(jnp.add, grads_sum, weight_grads)
        return ((grads_sum, jnp.maximum(top_scores, maxima)), (outputs, input_grads))
    start_max = jnp.full((HEADS,), very_low, jnp.float32)
    (grads, top_scores), (outputs, input_grads) = lax.scan(one_sequence, (zero_grads, start_max), (inputs, cotangents, segment_ids))
    grad_scale = lax.rsqrt(jnp.float32(TOKENS))
    step_value = jnp.float32(ADAM_STEP)
    moment_set = (qkv_moments, out_moments, up_moments, down_moments, gain_moments, bias_moments, up_bias_moments)
    results = [adam_update(param, moments, grad * grad_scale, step_value) for param, moments, grad in zip(weight_set, moment_set, grads)]
    factor = jnp.sqrt(clip_tau / jnp.maximum(top_scores, clip_tau))
    column = jnp.repeat(factor, HEAD_DIM)
    scales = jnp.stack([column, column, jnp.ones_like(column)])[:, None, :]
    new_qkv = results[0][0] * scales
    return (outputs.reshape(TOKENS, D).astype(jnp.bfloat16), input_grads.reshape(TOKENS, D), new_qkv, results[1][0], results[2][0], results[3][0], results[4][0], results[5][0], results[6][0], results[0][1], results[1][1], results[2][1], results[3][1], results[4][1], results[5][1], results[6][1])
```

```python
import functools

import jax
import jax.numpy as jnp
from jax import lax
from jax.experimental import pallas as pl
from jax.experimental.pallas import tpu as pltpu
from jax.sharding import PartitionSpec as P

HEADS = 16
HEAD_DIM = 64
ADAM_STEP = 5
PAIR = 2 * HEAD_DIM
LOG2E = 1.4426950408889634

very_low = -1e30
clip_tau = 5.0
learn_rate = 0.25
weight_decay = 0.1
moment_beta = 0.5
adam_epsilon = 1e-08


def norm_rows(values, gain_row, shift_row):
    center = values - jnp.mean(values, axis=-1, keepdims=True)
    spread = jnp.mean(center * center, axis=-1, keepdims=True)
    return center * lax.rsqrt(spread + 1e-05) * gain_row + shift_row


def gelu_exact(values):
    return jax.nn.gelu(values, approximate=False)


def times_transposed(left_side, right_side):
    return lax.dot_general(
        left_side, right_side, (((1,), (1,)), ((), ())), preferred_element_type=jnp.float32
    )


def transposed_times(left_side, right_side):
    return lax.dot_general(
        left_side, right_side, (((0,), (0,)), ((), ())), preferred_element_type=jnp.float32
    )


def adam_update(param, moments, grad, step_value):
    first_moment = moment_beta * moments[0] + (1.0 - moment_beta) * grad
    second_moment = moment_beta * moments[1] + (1.0 - moment_beta) * grad * grad
    correct = 1.0 - jnp.power(moment_beta, step_value)
    update = first_moment / correct / (jnp.sqrt(second_moment / correct) + adam_epsilon)
    return (
        param - learn_rate * (update + weight_decay * param),
        jnp.stack([first_moment, second_moment]),
    )


def place_columns(values, column_start, full_width):
    return lax.dynamic_update_slice_in_dim(
        jnp.zeros((full_width,), jnp.float32), values, column_start, 0
    )


bf=jnp.bfloat16
f32=jnp.float32
NN=(((1,),(0,)),((),()))
def dot(a,b): return lax.dot_general(a,b,NN,preferred_element_type=f32)

def fwd_kernel(BQ,CH,T, k_cur,k_nxt,q_cur,q_nxt,sq_cur,sq_nxt,vT, p_ref,o_ref,l_ref,m_ref, sA,sB,mA,mB):
    i=pl.program_id(0)
    zeros=jnp.zeros((64,BQ),bf)
    C1=f32(LOG2E*HEAD_DIM**-0.5)
    def aug(q_ref,sq,h):
        q=q_ref[h*64:(h+1)*64,:]
        parts=[q,zeros] if h==0 else [zeros,q]
        return jnp.concatenate(parts+[sq[...]],axis=0)
    def scores(ks,qa,s_ref,c,mx):
        st=dot(ks[c*CH:(c+1)*CH,:],qa)
        s_ref[c*CH:(c+1)*CH,:]=st
        return jnp.maximum(mx,jnp.max(st.reshape(CH//8,8,BQ),axis=0))
    def finish(mx,m_s):
        m_s[...]=jnp.broadcast_to(jnp.max(mx,axis=0,keepdims=True),(8,BQ))
    neg=jnp.full((8,BQ),-3e38,f32)
    n=T//CH
    @pl.when(i==0)
    def _():
        qa=aug(q_cur,sq_cur,0)
        mx=neg
        for c in range(n): mx=scores(k_cur,qa,sA,c,mx)
        finish(mx,mA)
    def phase(h,s_in,m_in,ks,qa,s_out,m_out):
        m=m_in[...]
        m1=m[0:1]
        mx=neg
        ls=jnp.zeros((8,BQ),f32)
        acc=jnp.zeros((64,BQ),f32)
        for c in range(n):
            mx=scores(ks,qa,s_out,c,mx)
            p=jnp.exp2((s_in[c*CH:(c+1)*CH,:]-m1)*C1)
            ls=ls+jnp.sum(p.reshape(CH//8,8,BQ),axis=0)
            pb=p.astype(bf)
            p_ref[0,h,0,c*CH:(c+1)*CH,:]=pb
            acc=acc+dot(vT[h*64:(h+1)*64,c*CH:(c+1)*CH],pb)
        finish(mx,m_out)
        l=jnp.sum(ls,axis=0,keepdims=True)
        o_ref[h*64:(h+1)*64,:]=acc/l
        l_ref[0,h:h+1,:]=l
        m_ref[0,h:h+1,:]=m1
    phase(0,sA,mA,k_cur,aug(q_cur,sq_cur,1),sB,mB)
    phase(1,sB,mB,k_nxt,aug(q_nxt,sq_nxt,0),sA,mA)

def attention_fwd(kaug,qT,sq,vT,BQ=256,CH=512):
    pairs,T,_=kaug.shape
    nq=T//BQ
    N=pairs*nq
    cur=lambda i:i
    nxt=lambda i:jnp.minimum(i+1,N-1)
    def km(f): return pl.BlockSpec((None,T,256),lambda i:(f(i)//nq,0,0))
    def qm(f): return pl.BlockSpec((128,BQ),lambda i:(f(i)//nq,f(i)%nq))
    def sm(f): return pl.BlockSpec((128,BQ),lambda i:(0,f(i)%nq))
    H=2*pairs
    return pl.pallas_call(
        functools.partial(fwd_kernel,BQ,CH,T),
        grid=(N,),
        in_specs=[km(cur),km(nxt),qm(cur),qm(nxt),sm(cur),sm(nxt),pl.BlockSpec((128,T),lambda i:(i//nq,0))],
        out_specs=[pl.BlockSpec((1,2,1,T,BQ),lambda i:(i//nq,0,i%nq,0,0)),
                   pl.BlockSpec((128,BQ),lambda i:(i//nq,i%nq)),
                   pl.BlockSpec((1,2,BQ),lambda i:(i//nq,0,i%nq)),
                   pl.BlockSpec((1,2,BQ),lambda i:(i//nq,0,i%nq))],
        out_shape=[jax.ShapeDtypeStruct((pairs,2,nq,T,BQ),bf),
                   jax.ShapeDtypeStruct((pairs*128,T),f32),
                   jax.ShapeDtypeStruct((pairs,2,T),f32),
                   jax.ShapeDtypeStruct((pairs,2,T),f32)],
        scratch_shapes=[pltpu.VMEM((T,BQ),f32),pltpu.VMEM((T,BQ),f32),pltpu.VMEM((8,BQ),f32),pltpu.VMEM((8,BQ),f32)],
        compiler_params=pltpu.CompilerParams(vmem_limit_bytes=58*2**20,dimension_semantics=("arbitrary",)),
        cost_estimate=pl.CostEstimate(flops=4*H*T*T*64*4,bytes_accessed=2*H*T*T,transcendentals=H*T*T),
    )(kaug,kaug,qT,qT,sq,sq,vT)

def bwd_kernel(BQ,CH,T, p_ref,doT,do,q,v,kT,dl, dq_ref,dk_ref,dv_ref):
    j=pl.program_id(0)
    @pl.when(j==0)
    def _():
        dk_ref[...]=jnp.zeros_like(dk_ref)
        dv_ref[...]=jnp.zeros_like(dv_ref)
    zeros=jnp.zeros((64,BQ),bf)
    zl=jnp.zeros((BQ,64),bf)
    def diag(x):
        x=x[...]
        lane=lax.broadcasted_iota(jnp.int32,(BQ,128),1)
        zz=jnp.zeros_like(x)
        return jnp.concatenate([jnp.where(lane<64,x,zz),jnp.where(lane>=64,x,zz)],axis=0)
    dod=diag(do); qd=diag(q)
    doTs=[jnp.concatenate([doT[0:64,:],zeros],0),jnp.concatenate([zeros,doT[64:128,:]],0)]
    dls=[dl[0,0:1,:],dl[0,1:2,:]]
    dqs=[jnp.zeros((64,BQ),f32) for _ in range(2)]
    for c in range(T//CH):
        sl=slice(c*CH,(c+1)*CH)
        vc=v[sl,:]
        ps=[];dss=[]
        for h in range(2):
            dp=dot(vc,doTs[h])
            p=p_ref[0,h,0,sl,:]
            ds=(p.astype(f32)*(dp-dls[h])).astype(bf)
            ps.append(p);dss.append(ds)
            dqs[h]=dqs[h]+dot(kT[h*64:(h+1)*64,sl],ds)
        dv_ref[sl,:]+=dot(jnp.concatenate(ps,1),dod)
        dk_ref[sl,:]+=dot(jnp.concatenate(dss,1),qd)
    for h in range(2):
        dq_ref[h*64:(h+1)*64,:]=dqs[h]*f32(HEAD_DIM**-0.5)
    @pl.when(j==pl.num_programs(0)-1)
    def _():
        dk_ref[...]=dk_ref[...]*f32(HEAD_DIM**-0.5)

def attention_bwd(p,doT,do,q,v,kT,dl,at,CH=1536):
    _,_,nq,T,BQ=p.shape
    CH=min(CH,T)
    return pl.pallas_call(
        functools.partial(bwd_kernel,BQ,CH,T),
        grid=(nq,),
        in_specs=[pl.BlockSpec((1,2,1,T,BQ),lambda j:(at,0,j,0,0)),
                  pl.BlockSpec((128,BQ),lambda j:(0,j)),
                  pl.BlockSpec((BQ,128),lambda j:(j,0)),
                  pl.BlockSpec((BQ,128),lambda j:(j,0)),
                  pl.BlockSpec((T,128),lambda j:(0,0)),
                  pl.BlockSpec((128,T),lambda j:(0,0)),
                  pl.BlockSpec((1,2,BQ),lambda j:(0,0,j))],
        out_specs=[pl.BlockSpec((128,BQ),lambda j:(0,j)),
                   pl.BlockSpec((T,128),lambda j:(0,0)),
                   pl.BlockSpec((T,128),lambda j:(0,0))],
        out_shape=[jax.ShapeDtypeStruct((128,T),f32),
                   jax.ShapeDtypeStruct((T,128),f32),
                   jax.ShapeDtypeStruct((T,128),f32)],
        compiler_params=pltpu.CompilerParams(vmem_limit_bytes=58*2**20,dimension_semantics=("arbitrary",)),
        cost_estimate=pl.CostEstimate(flops=8*2*T*T*64*4,bytes_accessed=2*2*T*T,transcendentals=0),
    )(p,doT,do,q,v,kT,dl)


def bits_of(size):
    return size.bit_length() - 1


def swap(value, axis_name, mask):
    size = lax.axis_size(axis_name)
    return lax.ppermute(value, axis_name, [(i, i ^ mask) for i in range(size)])


def pick(value, index, axis):
    return lax.dynamic_index_in_dim(value, index, axis, keepdims=False)


def halve(value, axis_name, bit, axis):
    mine = (lax.axis_index(axis_name) >> bit) & 1
    got = swap(pick(value, 1 - mine, axis).astype(jnp.bfloat16), axis_name, 1 << bit)
    return pick(value, mine, axis) + got.astype(jnp.float32)


def core_first(rows_t, right, add_axis=None):
    dp = lax.axis_size("dp")
    core = lax.axis_index("dp") & 1
    tokens = rows_t.shape[1]
    split = rows_t.reshape(dp // 2, 2, -1, tokens)
    other = pick(split, 1 - core, 1).reshape(-1, tokens)
    own = pick(split, core, 1).reshape(-1, tokens)
    sent = jnp.dot(other, right, preferred_element_type=jnp.float32).astype(jnp.bfloat16)
    got = swap(sent, "dp", 1)
    return jnp.dot(own, right, preferred_element_type=jnp.float32) + got.astype(jnp.float32)


def rest_of_dp(value):
    steps = bits_of(lax.axis_size("dp")) - 1
    width = value.shape[1]
    value = value.reshape((2,) * steps + (-1, width))
    for step in range(steps):
        value = halve(value, "dp", step + 1, steps - 1 - step)
    return value


def over_mp(value):
    steps = bits_of(lax.axis_size("mp"))
    rows, _, width = value.shape
    value = value.reshape((rows,) + (2,) * steps + (width,))
    for step in range(steps):
        value = halve(value, "mp", step, steps - step)
    return value


def over_mp_relative(blocks):
    blocks = list(blocks)
    for step in reversed(range(bits_of(len(blocks)))):
        size = 1 << step
        blocks = [
            blocks[j] + swap(blocks[j + size].astype(jnp.bfloat16), "mp", size).astype(jnp.float32)
            for j in range(size)
        ]
    return blocks[0]


def all_sum(value):
    for name in ("dp", "mp"):
        for step in range(bits_of(lax.axis_size(name))):
            value = value + swap(value, name, 1 << step)
    return value


def body(
    layer_input,
    out_cotangent,
    segment_ids,
    qkv_weight,
    out_weight,
    up_weight,
    down_weight,
    norm_gains,
    bias_rows,
    up_bias,
    qkv_moments,
    out_moments,
    up_moments,
    down_moments,
    gain_moments,
    bias_moments,
    up_bias_moments,
):
    mp = lax.axis_size("mp")
    me = lax.axis_index("mp")
    dp = lax.axis_size("dp")
    dp_me = lax.axis_index("dp")
    width = qkv_weight.shape[2]
    units = up_weight.shape[1]
    tokens, dim = layer_input.shape
    rows = tokens // mp
    pairs = width // PAIR
    heads_local = width // HEAD_DIM
    low = jnp.bfloat16
    block = min(512, tokens)
    column_start = me * width

    def relative(value, axis):
        shape = value.shape
        value = value.reshape(shape[:axis] + (mp, rows) + shape[axis + 1 :])
        parts = [pick(value, me ^ j, axis) for j in range(mp)]
        return jnp.concatenate(parts, axis=axis)

    qkv_low = qkv_weight.astype(low)
    qkv_full = lax.all_gather(qkv_low, "dp", axis=1, tiled=True)
    first_set = jnp.concatenate([out_weight.astype(low), up_weight.astype(low)], axis=1)
    second_set = jnp.concatenate(
        [down_weight.astype(low), qkv_low.transpose(1, 0, 2).reshape(-1, 3 * width)], axis=1
    )
    inputs = relative(layer_input, 0)
    inputs_t = inputs.T
    ids = relative(segment_ids.reshape(-1), 0)

    projected = jnp.einsum("td,cde->cte", inputs, qkv_full, preferred_element_type=jnp.float32)
    query_bias = lax.dynamic_slice_in_dim(bias_rows[0], column_start, width)
    value_bias = lax.dynamic_slice_in_dim(bias_rows[1], column_start, width)
    queries = (projected[0] + query_bias).astype(low)
    keys_all = projected[1].astype(low)
    values_all = (projected[2] + value_bias).astype(low)
    queries_t = queries.T
    keys_t = keys_all.T
    values_t = values_all.T
    first_all = lax.all_gather(first_set, ("mp", "dp"), axis=0, tiled=True).reshape(mp, dim, -1)
    second_all = lax.all_gather(second_set, ("mp", "dp"), axis=0, tiled=True).reshape(mp, dim, -1)
    document = jnp.arange(PAIR, dtype=jnp.int32)
    same = ids[:, None] == document[None, :]
    key_marks = jnp.where(same | (document[None, :] > 2), 0.0, very_low).astype(low)
    query_marks = same.T.astype(low)
    key_rows = jnp.concatenate(
        [
            keys_all.reshape(tokens, pairs, PAIR).transpose(1, 0, 2),
            jnp.broadcast_to(key_marks[None], (pairs, tokens, PAIR)),
        ],
        axis=-1,
    )

    calls = 2 if pairs % 2 == 0 else 1
    per_call = pairs // calls
    probs, attended_t, totals, attended_rel = [], [], [], [[] for _ in range(mp)]
    tops = []
    for call in range(calls):
        span = slice(call * per_call * PAIR, (call + 1) * per_call * PAIR)
        call_probs, call_out, call_total, call_max = attention_fwd(
            key_rows[call * per_call : (call + 1) * per_call],
            queries_t[span],
            query_marks,
            values_t[span],
            BQ=block,
        )
        probs.append(call_probs)
        attended_t.append(call_out)
        totals.append(call_total)
        tops.append(jnp.max(call_max, axis=2).reshape(-1))
        call_low = call_out.astype(low)
        for j in range(mp):
            piece = call_low[:, j * rows : (j + 1) * rows]
            attended_rel[j].append(piece if j == 0 else swap(piece, "mp", j))
    head_max = jnp.concatenate(tops) * HEAD_DIM ** (-0.5)
    attended_rel = [jnp.concatenate(parts, axis=0) for parts in attended_rel]

    out_full, up_full = first_all[:, :, :width], first_all[:, :, width:]
    down_full, qkv_other = second_all[:, :, :units], second_all[:, :, units:]
    out_rel = [pick(out_full, me ^ j, 0) for j in range(mp)]
    branch = 0.0
    for j in range(mp):
        branch = branch + lax.dot_general(
            attended_rel[j],
            out_rel[j],
            (((0,), (1,)), ((), ())),
            preferred_element_type=jnp.float32,
        )
    summed = inputs[:rows].astype(jnp.float32) + branch + bias_rows[2]
    normed, first_norm_pull = jax.vjp(norm_rows, summed, norm_gains[0], bias_rows[4])
    normed_low = normed.astype(low)
    pre_act = jnp.concatenate(
        [jnp.dot(normed_low, up_full[m], preferred_element_type=jnp.float32) for m in range(mp)],
        axis=1,
    )
    pre_act = pre_act + up_bias
    hidden, gelu_pull = jax.vjp(gelu_exact, pre_act)
    hidden_low = hidden.astype(low)
    ffn_out = 0.0
    for m in range(mp):
        ffn_out = ffn_out + times_transposed(
            hidden_low[:, m * units : (m + 1) * units], down_full[m]
        )
    total = normed + ffn_out + bias_rows[3]
    result, second_norm_pull = jax.vjp(norm_rows, total, norm_gains[1], bias_rows[5])
    total_grad, second_gain_grad, second_shift_grad = second_norm_pull(
        out_cotangent.astype(jnp.float32)
    )
    total_low = total_grad.astype(low)
    down_part = core_first(total_low.T, hidden_low)
    hidden_grad = jnp.concatenate(
        [jnp.dot(total_low, down_full[m], preferred_element_type=jnp.float32) for m in range(mp)],
        axis=1,
    )
    pre_grad = gelu_pull(hidden_grad)[0]
    up_bias_grad = jnp.sum(pre_grad, axis=0)
    pre_low = pre_grad.astype(low)
    up_part = core_first(normed_low.T, pre_low)
    normed_grad = total_grad
    for m in range(mp):
        normed_grad = normed_grad + times_transposed(
            pre_low[:, m * units : (m + 1) * units], up_full[m]
        )
    summed_grad, first_gain_grad, first_shift_grad = first_norm_pull(normed_grad)
    summed_low = summed_grad.astype(low)
    grad_rel = []
    for j in range(mp):
        piece = jnp.dot(summed_low, out_rel[j], preferred_element_type=jnp.float32).astype(low)
        grad_rel.append(piece if j == 0 else swap(piece, "mp", j))
    attended_grad = jnp.concatenate(grad_rel, axis=0)
    out_part = core_first(summed_low.T, jnp.concatenate(attended_rel, axis=0).T)

    down_sum = over_mp(rest_of_dp(down_part).reshape(-1, mp, units))
    up_sum = over_mp(rest_of_dp(up_part).reshape(-1, mp, units))
    out_sum = rest_of_dp(out_part)
    out_sum = over_mp_relative([out_sum[:, j * width : (j + 1) * width] for j in range(mp)])

    slots = lax.dynamic_update_slice_in_dim(
        jnp.zeros((dp * mp, heads_local), jnp.float32),
        head_max[None],
        dp_me * mp + me,
        0,
    )
    early = all_sum(
        jnp.concatenate(
            [
                first_gain_grad,
                second_gain_grad,
                jnp.sum(summed_grad, axis=0),
                jnp.sum(total_grad, axis=0),
                first_shift_grad,
                second_shift_grad,
                up_bias_grad,
                slots.reshape(-1),
            ]
        )
    )
    gain_sum = early[: 2 * dim].reshape(2, dim)
    late_biases = early[2 * dim : 6 * dim].reshape(4, dim)
    unit_sum = early[6 * dim : 6 * dim + units * mp]
    group_max = jnp.max(early[6 * dim + units * mp :].reshape(dp, mp, heads_local), axis=0)
    local_max = pick(group_max, me, 0)

    inverse = 1.0 / jnp.concatenate(totals, axis=0).reshape(heads_local, tokens)
    grad_t = attended_grad.T
    scaled = (
        attended_grad.astype(jnp.float32).reshape(tokens, heads_local, HEAD_DIM)
        * inverse.T[:, :, None]
    )
    scaled = scaled.reshape(tokens, width).astype(low)
    scaled_t = scaled.T
    delta = jnp.sum(
        (grad_t.astype(jnp.float32) * jnp.concatenate(attended_t, axis=0)).reshape(
            heads_local, HEAD_DIM, tokens
        ),
        axis=1,
    )
    delta = (delta * inverse).reshape(pairs, 2, tokens)
    own_rows, got_rows = [], [[] for _ in range(mp - 1)]
    qkv_pieces, bias_pieces = [], []
    for pair in range(pairs):
        span = slice(pair * PAIR, (pair + 1) * PAIR)
        call, at = pair // per_call, pair % per_call
        query_grad, key_grad, value_grad = attention_bwd(
            probs[call],
            scaled_t[span],
            scaled[:, span],
            queries[:, span],
            values_all[:, span],
            keys_t[span],
            delta[pair : pair + 1],
            at,
        )
        bias_pieces.append(jnp.stack([jnp.sum(query_grad, axis=1), jnp.sum(value_grad, axis=0)]))
        grads_low = jnp.concatenate(
            [query_grad.T.astype(low), key_grad.astype(low), value_grad.astype(low)], axis=1
        )
        own_rows.append(grads_low[:rows])
        for j in range(1, mp):
            got_rows[j - 1].append(swap(grads_low[j * rows : (j + 1) * rows], "mp", j))
        qkv_pieces.append(core_first(inputs_t, grads_low))
    qkv_sums = [rest_of_dp(piece) for piece in qkv_pieces]

    def by_pair(weights):
        weights = weights.reshape(dim, 3, pairs, PAIR).transpose(0, 2, 1, 3)
        return weights.reshape(dim, 3 * width)

    input_grad = summed_grad + times_transposed(
        jnp.concatenate(own_rows, axis=1), by_pair(qkv_full.transpose(1, 0, 2))
    )
    for j in range(1, mp):
        input_grad = input_grad + times_transposed(
            jnp.concatenate(got_rows[j - 1], axis=1), by_pair(pick(qkv_other, me ^ j, 0))
        )
    qkv_sum = jnp.concatenate(
        [piece.reshape(-1, 3, 1, PAIR) for piece in qkv_sums], axis=2
    ).reshape(-1, 3, width)
    qkv_sum = qkv_sum.transpose(1, 0, 2)
    head_biases = jnp.concatenate(bias_pieces, axis=1)
    head_biases = lax.dynamic_update_slice_in_dim(
        jnp.zeros((2, width * mp), jnp.float32), head_biases, column_start, 1
    )
    bias_sum = jnp.concatenate([all_sum(head_biases), late_biases], axis=0)

    grad_scale = lax.rsqrt(jnp.float32(tokens * dp))
    step_value = jnp.float32(ADAM_STEP)
    new_qkv, next_qkv = adam_update(qkv_weight, qkv_moments, qkv_sum * grad_scale, step_value)
    new_out, next_out = adam_update(out_weight, out_moments, out_sum * grad_scale, step_value)
    new_up, next_up = adam_update(up_weight, up_moments, up_sum * grad_scale, step_value)
    new_down, next_down = adam_update(down_weight, down_moments, down_sum * grad_scale, step_value)
    new_gains, next_gains = adam_update(norm_gains, gain_moments, gain_sum * grad_scale, step_value)
    new_biases, next_biases = adam_update(
        bias_rows, bias_moments, bias_sum * grad_scale, step_value
    )
    new_up_bias, next_up_bias = adam_update(
        up_bias, up_bias_moments, unit_sum * grad_scale, step_value
    )
    factor = jnp.sqrt(clip_tau / jnp.maximum(local_max, clip_tau))
    column = jnp.repeat(factor, HEAD_DIM)
    scales = jnp.stack([column, column, jnp.ones_like(column)])[:, None, :]
    new_qkv = new_qkv * scales
    return (
        result.astype(jnp.bfloat16),
        input_grad,
        new_qkv,
        new_out,
        new_up,
        new_down,
        new_gains,
        new_biases,
        new_up_bias,
        next_qkv,
        next_out,
        next_up,
        next_down,
        next_gains,
        next_biases,
        next_up_bias,
    )


def solution(mesh):
    placed = (
        P("dp", None),
        P(("dp", "mp"), None),
        P("dp", None),
        P(None, "dp", "mp"),
        P("dp", "mp"),
        P("dp", "mp"),
        P("dp", "mp"),
        P(),
        P(),
        P(),
        P(None, None, "dp", "mp"),
        P(None, "dp", "mp"),
        P(None, "dp", "mp"),
        P(None, "dp", "mp"),
        P(),
        P(),
        P(),
    )
    return jax.shard_map(
        body,
        mesh=mesh,
        in_specs=placed,
        out_specs=(
            P(("dp", "mp"), None),
            P(("dp", "mp"), None),
            P(None, "dp", "mp"),
            P("dp", "mp"),
            P("dp", "mp"),
            P("dp", "mp"),
            P(),
            P(),
            P(),
            P(None, None, "dp", "mp"),
            P(None, "dp", "mp"),
            P(None, "dp", "mp"),
            P(None, "dp", "mp"),
            P(),
            P(),
            P(),
        ),
        check_vma=False,
    )
```

```python
import functools

import jax
import jax.numpy as jnp
from jax import lax
from jax.experimental import pallas as pl
from jax.experimental.pallas import tpu as pltpu
from jax.sharding import PartitionSpec as P

HEAD_DIM = 64
ADAM_STEP = 5
PAIR = 2 * HEAD_DIM
LOG2E = 1.4426950408889634

low = jnp.bfloat16
f32 = jnp.float32
very_low = -1e30
clip_tau = 5.0
learn_rate = 0.25
weight_decay = 0.1
moment_beta = 0.5
adam_epsilon = 1e-08


def norm_rows(values, gain_row, shift_row):
    center = values - jnp.mean(values, axis=-1, keepdims=True)
    spread = jnp.mean(center * center, axis=-1, keepdims=True)
    return center * lax.rsqrt(spread + 1e-05) * gain_row + shift_row


def times_transposed(left_side, right_side):
    return lax.dot_general(
        left_side, right_side, (((1,), (1,)), ((), ())), preferred_element_type=jnp.float32
    )


def adam_update(param, moments, grad, step_value):
    first_moment = moment_beta * moments[0] + (1.0 - moment_beta) * grad
    second_moment = moment_beta * moments[1] + (1.0 - moment_beta) * grad * grad
    correct = 1.0 - jnp.power(moment_beta, step_value)
    update = first_moment / correct / (jnp.sqrt(second_moment / correct) + adam_epsilon)
    return (
        param - learn_rate * (update + weight_decay * param),
        jnp.stack([first_moment, second_moment]),
    )


def dot(left, right):
    return lax.dot_general(left, right, (((1,), (0,)), ((), ())), preferred_element_type=f32)


def dot_nt(left, right):
    return lax.dot_general(left, right, (((1,), (1,)), ((), ())), preferred_element_type=f32)


def kernel_params(axes=1):
    return pltpu.CompilerParams(
        vmem_limit_bytes=58 * 2**20, dimension_semantics=("arbitrary",) * axes
    )


def brief(flops):
    return pl.CostEstimate(flops=flops // 16, bytes_accessed=2**20, transcendentals=0)


def project_kernel(pairs, x, weights, biases, marks, q_ref, qt_ref, k_ref, kt_ref, v_ref, vt_ref):
    for pair in range(pairs):
        span = slice(pair * PAIR, (pair + 1) * PAIR)
        every = dot(x[...], weights[:, 3 * pair * PAIR : 3 * (pair + 1) * PAIR])
        q = every[:, :PAIR] + biases[0:1, span]
        k = every[:, PAIR : 2 * PAIR]
        v = every[:, 2 * PAIR :] + biases[1:2, span]
        q_ref[:, span] = q.astype(low)
        qt_ref[span, :] = q.T.astype(low)
        k_ref[pair, :, :PAIR] = k.astype(low)
        k_ref[pair, :, PAIR:] = marks[...]
        kt_ref[span, :] = k.T.astype(low)
        v_ref[:, span] = v.astype(low)
        vt_ref[span, :] = v.T.astype(low)


def project(x, weights, biases, marks):
    tokens, dim = x.shape
    width = weights.shape[1] // 3
    pairs = width // PAIR
    block = min(512, tokens)
    rows = lambda n: pl.BlockSpec((block, n), lambda i: (i, 0))
    columns = pl.BlockSpec((width, block), lambda i: (0, i))
    natural = jax.ShapeDtypeStruct((tokens, width), low)
    turned = jax.ShapeDtypeStruct((width, tokens), low)
    return pl.pallas_call(
        functools.partial(project_kernel, pairs),
        grid=(tokens // block,),
        in_specs=[
            rows(dim),
            pl.BlockSpec((dim, 3 * width), lambda i: (0, 0)),
            pl.BlockSpec((2, width), lambda i: (0, 0)),
            rows(PAIR),
        ],
        out_specs=[
            rows(width),
            columns,
            pl.BlockSpec((pairs, block, 2 * PAIR), lambda i: (0, i, 0)),
            columns,
            rows(width),
            columns,
        ],
        out_shape=[
            natural,
            turned,
            jax.ShapeDtypeStruct((pairs, tokens, 2 * PAIR), low),
            turned,
            natural,
            turned,
        ],
        compiler_params=kernel_params(),
        cost_estimate=brief(6 * tokens * dim * width),
        name="project",
    )(x, weights, biases, marks)


def forward_kernel(
    bq, ch, tokens, k_cur, k_nxt, q_cur, q_nxt, s_cur, s_nxt, vt,
    p_ref, ot_ref, o_ref, l_ref, m_ref, score_a, score_b, max_a, max_b,
):
    zeros = jnp.zeros((HEAD_DIM, bq), low)
    factor = f32(LOG2E * HEAD_DIM**-0.5)
    steps = tokens // ch
    nq = tokens // bq

    def query_rows(q_ref, marks, head):
        q = q_ref[head * HEAD_DIM : (head + 1) * HEAD_DIM, :]
        parts = [q, zeros] if head == 0 else [zeros, q]
        return jnp.concatenate(parts + [marks[...]], axis=0)

    def scores(keys, q, out, step, top):
        part = dot(keys[step * ch : (step + 1) * ch, :], q)
        out[step * ch : (step + 1) * ch, :] = part
        return jnp.maximum(top, jnp.max(part.reshape(ch // 8, 8, bq), axis=0))

    def finish(top, out):
        out[...] = jnp.broadcast_to(jnp.max(top, axis=0, keepdims=True), (8, bq))

    lowest = jnp.full((8, bq), -3e38, f32)

    @pl.when(pl.program_id(0) == 0)
    def _():
        q = query_rows(q_cur, s_cur, 0)
        top = lowest
        for step in range(steps):
            top = scores(k_cur, q, score_a, step, top)
        finish(top, max_a)

    def phase(head, s_in, m_in, keys, q, s_out, m_out):
        top_row = m_in[0:1, :]
        top = lowest
        sums = jnp.zeros((8, bq), f32)
        total = jnp.zeros((HEAD_DIM, bq), f32)
        for step in range(steps):
            span = slice(step * ch, (step + 1) * ch)
            top = scores(keys, q, s_out, step, top)
            p = jnp.exp2((s_in[span, :] - top_row) * factor)
            sums = sums + jnp.sum(p.reshape(ch // 8, 8, bq), axis=0)
            p_low = p.astype(low)
            p_ref[0, head, 0, span, :] = p_low
            total = total + dot(vt[head * HEAD_DIM : (head + 1) * HEAD_DIM, span], p_low)
        finish(top, m_out)
        row_sum = jnp.sum(sums, axis=0, keepdims=True)
        l_ref[0, head : head + 1, :] = row_sum
        best = top_row[:, :PAIR]
        for first in range(PAIR, bq, PAIR):
            best = jnp.maximum(best, top_row[:, first : first + PAIR])
        here = jnp.where(pl.program_id(0) % nq == 0, lowest[0:1, :PAIR], m_ref[0, head : head + 1, :])
        m_ref[0, head : head + 1, :] = jnp.maximum(here, best)
        return total / row_sum

    first = phase(0, score_a, max_a, k_cur, query_rows(q_cur, s_cur, 1), score_b, max_b)
    second = phase(1, score_b, max_b, k_nxt, query_rows(q_nxt, s_nxt, 0), score_a, max_a)
    both = jnp.concatenate([first, second], axis=0)
    ot_ref[...] = both
    o_ref[...] = both.T.astype(low)


def attention_forward(keys, q_t, marks_t, v_t, first, pairs, bq, ch=512):
    _, tokens, _ = keys.shape
    nq = tokens // bq
    ch = min(ch, tokens)
    count = pairs * nq
    now = lambda i: i
    later = lambda i: jnp.minimum(i + 1, count - 1)
    key_spec = lambda at: pl.BlockSpec(
        (None, tokens, 2 * PAIR), lambda i: (first + at(i) // nq, 0, 0)
    )
    query_spec = lambda at: pl.BlockSpec((PAIR, bq), lambda i: (first + at(i) // nq, at(i) % nq))
    mark_spec = lambda at: pl.BlockSpec((PAIR, bq), lambda i: (0, at(i) % nq))
    row_spec = pl.BlockSpec((1, 2, bq), lambda i: (i // nq, 0, i % nq))
    size = 2 * pairs * tokens * tokens
    return pl.pallas_call(
        functools.partial(forward_kernel, bq, ch, tokens),
        grid=(count,),
        in_specs=[
            key_spec(now), key_spec(later), query_spec(now), query_spec(later),
            mark_spec(now), mark_spec(later),
            pl.BlockSpec((PAIR, tokens), lambda i: (first + i // nq, 0)),
        ],
        out_specs=[
            pl.BlockSpec((1, 2, 1, tokens, bq), lambda i: (i // nq, 0, i % nq, 0, 0)),
            pl.BlockSpec((PAIR, bq), lambda i: (i // nq, i % nq)),
            pl.BlockSpec((bq, PAIR), lambda i: (i % nq, i // nq)),
            row_spec,
            pl.BlockSpec((1, 2, PAIR), lambda i: (i // nq, 0, 0)),
        ],
        out_shape=[
            jax.ShapeDtypeStruct((pairs, 2, nq, tokens, bq), low),
            jax.ShapeDtypeStruct((pairs * PAIR, tokens), f32),
            jax.ShapeDtypeStruct((tokens, pairs * PAIR), low),
            jax.ShapeDtypeStruct((pairs, 2, tokens), f32),
            jax.ShapeDtypeStruct((pairs, 2, PAIR), f32),
        ],
        scratch_shapes=[
            pltpu.VMEM((tokens, bq), f32),
            pltpu.VMEM((tokens, bq), f32),
            pltpu.VMEM((8, bq), f32),
            pltpu.VMEM((8, bq), f32),
        ],
        compiler_params=kernel_params(),
        cost_estimate=brief(16 * HEAD_DIM * size),
        name="attend",
    )(keys, keys, q_t, q_t, marks_t, marks_t, v_t)


def backward_kernel(
    bq, ch, tokens, p_ref, grad, out_t, totals, q, v, kt, g_ref, b_ref, key_acc, value_acc, sums
):
    step_q = pl.program_id(0)

    @pl.when(step_q == 0)
    def _():
        key_acc[...] = jnp.zeros_like(key_acc)
        value_acc[...] = jnp.zeros_like(value_acc)
        sums[...] = jnp.zeros_like(sums)

    zeros = jnp.zeros((HEAD_DIM, bq), low)
    scale = f32(HEAD_DIM**-0.5)
    lane = lax.broadcasted_iota(jnp.int32, (bq, PAIR), 1)

    def diagonal(x):
        zero = jnp.zeros_like(x)
        return jnp.concatenate(
            [jnp.where(lane < HEAD_DIM, x, zero), jnp.where(lane >= HEAD_DIM, x, zero)], axis=0
        )

    grad_t = grad[...].astype(f32).T
    scaled_t, deltas = [], []
    for head in range(2):
        inverse = 1.0 / totals[0, head : head + 1, :]
        span = slice(head * HEAD_DIM, (head + 1) * HEAD_DIM)
        part = grad_t[span] * inverse
        deltas.append(jnp.sum(part * out_t[span, :], axis=0, keepdims=True))
        scaled_t.append(part)
    scaled = jnp.concatenate(scaled_t, axis=0).T.astype(low)
    grad_rows = diagonal(scaled)
    query_rows = diagonal(q[...])
    grad_columns = [
        jnp.concatenate([scaled_t[0].astype(low), zeros], axis=0),
        jnp.concatenate([zeros, scaled_t[1].astype(low)], axis=0),
    ]
    query_grads = [jnp.zeros((HEAD_DIM, bq), f32) for _ in range(2)]
    for step in range(tokens // ch):
        span = slice(step * ch, (step + 1) * ch)
        values = v[span, :]
        probs, score_grads = [], []
        for head in range(2):
            prob_grad = dot(values, grad_columns[head])
            p = p_ref[0, head, 0, span, :]
            score_grad = (p.astype(f32) * (prob_grad - deltas[head])).astype(low)
            probs.append(p)
            score_grads.append(score_grad)
            query_grads[head] = query_grads[head] + dot(
                kt[head * HEAD_DIM : (head + 1) * HEAD_DIM, span], score_grad
            )
        value_acc[span, :] += dot(jnp.concatenate(probs, axis=1), grad_rows)
        key_acc[span, :] += dot(jnp.concatenate(score_grads, axis=1), query_rows)
    query_grad = jnp.concatenate(query_grads, axis=0).T * scale
    g_ref[pl.ds(pl.multiple_of(step_q * bq, bq), bq), 0:PAIR] = query_grad.astype(low)
    sums[...] += jnp.sum(query_grad.reshape(bq // 8, 8, PAIR), axis=0)

    @pl.when(step_q == pl.num_programs(0) - 1)
    def _():
        g_ref[:, PAIR : 2 * PAIR] = (key_acc[...] * scale).astype(low)
        value_grad = value_acc[...]
        g_ref[:, 2 * PAIR :] = value_grad.astype(low)
        b_ref[0:1, :] = jnp.sum(sums[...], axis=0, keepdims=True)
        b_ref[1:2, :] = jnp.sum(value_grad, axis=0, keepdims=True)


def attention_backward(probs, grad, out_t, totals, q, v, k_t, pair, at, ch=1536):
    _, _, nq, tokens, bq = probs.shape
    ch = min(ch, tokens)
    size = 2 * tokens * tokens
    return pl.pallas_call(
        functools.partial(backward_kernel, bq, ch, tokens),
        grid=(nq,),
        in_specs=[
            pl.BlockSpec((1, 2, 1, tokens, bq), lambda i: (at, 0, i, 0, 0)),
            pl.BlockSpec((bq, PAIR), lambda i: (i, 0)),
            pl.BlockSpec((PAIR, bq), lambda i: (at, i)),
            pl.BlockSpec((1, 2, bq), lambda i: (at, 0, i)),
            pl.BlockSpec((bq, PAIR), lambda i: (i, pair)),
            pl.BlockSpec((tokens, PAIR), lambda i: (0, pair)),
            pl.BlockSpec((PAIR, tokens), lambda i: (pair, 0)),
        ],
        out_specs=[
            pl.BlockSpec((tokens, 3 * PAIR), lambda i: (0, 0)),
            pl.BlockSpec((2, PAIR), lambda i: (0, 0)),
        ],
        out_shape=[
            jax.ShapeDtypeStruct((tokens, 3 * PAIR), low),
            jax.ShapeDtypeStruct((2, PAIR), f32),
        ],
        scratch_shapes=[
            pltpu.VMEM((tokens, PAIR), f32),
            pltpu.VMEM((tokens, PAIR), f32),
            pltpu.VMEM((8, PAIR), f32),
        ],
        compiler_params=kernel_params(),
        cost_estimate=brief(32 * HEAD_DIM * size),
        name="attend_back",
    )(probs, grad, out_t, totals, q, v, k_t)


def gelu_and_slope(x):
    size = jnp.abs(x) * f32(0.7071067811865476)
    t = 1.0 / (1.0 + f32(0.3275911) * size)
    bell = jnp.exp2(x * x * f32(-0.5 * LOG2E))
    poly = f32(1.061405429 / 2)
    for coefficient in (-1.453152027, 1.421413741, -0.284496736, 0.254829592):
        poly = poly * t + f32(coefficient / 2)
    tail = poly * t * bell
    phi = jnp.where(x >= 0, 1.0 - tail, tail)
    return x * phi, phi + x * bell * f32(0.3989422804014327)


def feed_kernel(rows, ch, x, up, down, bias, hidden_ref, slope_ref, out_ref):
    @pl.when(pl.program_id(0) == 0)
    def _():
        out_ref[...] = jnp.zeros_like(out_ref)

    def finish(span, pre):
        hidden, slope = gelu_and_slope(pre + bias[...])
        hidden = hidden.astype(low)
        hidden_ref[span, :] = hidden
        slope_ref[span, :] = slope.astype(low)
        out_ref[span, :] += dot_nt(hidden, down[...])

    before = None
    for first in range(0, rows, ch):
        span = slice(first, first + ch)
        pre = dot(x[span, :], up[...])
        if before is not None:
            finish(*before)
        before = (span, pre)
    finish(*before)


def feed_forward(x, weights, bias, units, block=1024, ch=512):
    rows, dim = x.shape
    groups = weights.shape[0]
    block = min(block, units)
    per = units // block
    ch = ch if rows % ch == 0 else rows
    every = groups * units
    weight = lambda skip: pl.BlockSpec(
        (None, dim, block), lambda i: (i // per, 0, skip * per + i % per)
    )
    part = pl.BlockSpec((rows, block), lambda i: (0, i))
    whole = pl.BlockSpec((rows, dim), lambda i: (0, 0))
    return pl.pallas_call(
        functools.partial(feed_kernel, rows, ch),
        grid=(groups * per,),
        in_specs=[whole, weight(0), weight(1), pl.BlockSpec((1, block), lambda i: (0, i))],
        out_specs=[part, part, whole],
        out_shape=[
            jax.ShapeDtypeStruct((rows, every), low),
            jax.ShapeDtypeStruct((rows, every), low),
            jax.ShapeDtypeStruct((rows, dim), f32),
        ],
        compiler_params=kernel_params(),
        cost_estimate=brief(4 * rows * dim * every),
        name="feed",
    )(x, weights, weights, bias)


def feed_back_kernel(
    rows, ch, blocks, core, x, normed, up, down, slope, hidden,
    sum_ref, out_ref, sent_ref, own_ref, x_t, normed_t, pre_all,
):
    half = x_t.shape[0] // 2
    size = 2 * half // blocks

    @pl.when(pl.program_id(0) == 0)
    def _():
        out_ref[...] = jnp.zeros_like(out_ref)
        for source, turned in ((x, x_t), (normed, normed_t)):
            for first in range(0, blocks, 2):
                pair = source[:, first * size : (first + 2) * size].T
                for odd in range(2):
                    own = jnp.where(core[0] == odd, half, 0)
                    at = pl.multiple_of(own + first // 2 * size, size)
                    turned[pl.ds(at, size), :] = pair[odd * size : (odd + 1) * size]

    block = slope.shape[1]
    sums = jnp.zeros((8, block), f32)

    def finish(span, hidden_grad, sums):
        pre = hidden_grad * slope[span, :].astype(f32)
        sums = sums + jnp.sum(pre.reshape(ch // 8, 8, block), axis=0)
        pre = pre.astype(low)
        pre_all[span, :] = pre
        out_ref[span, :] += dot_nt(pre, up[...])
        return sums

    before = None
    for first in range(0, rows, ch):
        span = slice(first, first + ch)
        hidden_grad = dot(x[span, :], down[...])
        if before is not None:
            sums = finish(*before, sums)
        before = (span, hidden_grad)
    owners = (blocks // 2, size, block)
    sent_ref[:, 1] = dot(x_t[:half, :], hidden[...]).astype(low).reshape(owners)
    sums = finish(*before, sums)
    sum_ref[...] = jnp.sum(sums, axis=0, keepdims=True)
    own_ref[:, 1] = dot(x_t[half:, :], hidden[...]).reshape(owners)
    sent_ref[:, 0] = dot(normed_t[:half, :], pre_all[...]).astype(low).reshape(owners)
    own_ref[:, 0] = dot(normed_t[half:, :], pre_all[...]).reshape(owners)


def feed_back(core, blocks, x, normed, weights, slope, hidden, units, block=512, ch=512):
    rows, dim = x.shape
    groups = weights.shape[0]
    block = min(block, units)
    per = units // block
    ch = ch if rows % ch == 0 else rows
    every = groups * units
    weight = lambda skip: pl.BlockSpec(
        (None, dim, block), lambda i: (i // per, 0, skip * per + i % per)
    )
    part = pl.BlockSpec((rows, block), lambda i: (0, i))
    owners = (blocks // 2, 2, dim // blocks)
    half = pl.BlockSpec(owners + (block,), lambda i: (0, 0, 0, i))
    once = pl.BlockSpec((rows, dim), lambda i: (0, 0), pipeline_mode=pl.Buffered(1))
    return pl.pallas_call(
        functools.partial(feed_back_kernel, rows, ch, blocks),
        grid=(groups * per,),
        in_specs=[
            pl.BlockSpec(memory_space=pltpu.SMEM), once, once, weight(0), weight(1), part, part
        ],
        out_specs=[
            pl.BlockSpec((1, block), lambda i: (0, i)),
            pl.BlockSpec((rows, dim), lambda i: (0, 0)),
            half,
            half,
        ],
        out_shape=[
            jax.ShapeDtypeStruct((1, every), f32),
            jax.ShapeDtypeStruct((rows, dim), f32),
            jax.ShapeDtypeStruct(owners + (every,), low),
            jax.ShapeDtypeStruct(owners + (every,), f32),
        ],
        scratch_shapes=[
            pltpu.VMEM((dim, rows), low),
            pltpu.VMEM((dim, rows), low),
            pltpu.VMEM((rows, block), low),
        ],
        compiler_params=kernel_params(),
        cost_estimate=brief(8 * rows * dim * every),
        name="feed_back",
    )(core, x, normed, weights, weights, slope, hidden)


def bits_of(size):
    return size.bit_length() - 1


def swap(value, axis_name, mask):
    size = lax.axis_size(axis_name)
    return lax.ppermute(value, axis_name, [(i, i ^ mask) for i in range(size)])


def pick(value, index, axis):
    return lax.dynamic_index_in_dim(value, index, axis, keepdims=False)


def after(value, *others):
    return lax.optimization_barrier((value,) + others)[0]


def halve_parts(value, axis_name, bit, axis):
    mine = (lax.axis_index(axis_name) >> bit) & 1
    return pick(value, 1 - mine, axis).astype(jnp.bfloat16), pick(value, mine, axis)


def halve(value, axis_name, bit, axis):
    sent, kept = halve_parts(value, axis_name, bit, axis)
    return kept + swap(sent, axis_name, 1 << bit).astype(jnp.float32)


def chip_steps():
    return bits_of(lax.axis_size("dp")) - 1


def by_bits(value):
    return value.reshape((2,) * chip_steps() + (-1, value.shape[-1]))


def core_halves(rows_t):
    core = lax.axis_index("dp") & 1
    tokens = rows_t.shape[1]
    split = rows_t.reshape(lax.axis_size("dp") // 2, 2, -1, tokens)
    return pick(split, 1 - core, 1).reshape(-1, tokens), pick(split, core, 1).reshape(-1, tokens)


def core_first(halves, right):
    other, own = halves
    sent = jnp.dot(other, right, preferred_element_type=jnp.float32).astype(jnp.bfloat16)
    got = swap(sent, "dp", 1)
    return jnp.dot(own, right, preferred_element_type=jnp.float32) + got.astype(jnp.float32)


def over_chips(value):
    dp = lax.axis_size("dp")
    groups = [[i for i in range(dp) if i % 2 == core] for core in range(2)]
    return lax.psum_scatter(
        value, "dp", scatter_dimension=0, axis_index_groups=groups, tiled=True
    )


def over_mp(value):
    steps = bits_of(lax.axis_size("mp"))
    rows, _, width = value.shape
    value = value.reshape((rows,) + (2,) * steps + (width,))
    for step in range(steps):
        value = halve(value, "mp", step, steps - step)
    return value


def over_mp_relative(blocks):
    blocks = list(blocks)
    for step in reversed(range(bits_of(len(blocks)))):
        size = 1 << step
        blocks = [
            blocks[j] + swap(blocks[j + size].astype(jnp.bfloat16), "mp", size).astype(jnp.float32)
            for j in range(size)
        ]
    return blocks[0]


def sum_steps():
    return [
        (name, 1 << step) for name in ("mp", "dp") for step in range(bits_of(lax.axis_size(name)))
    ]


def body(
    layer_input,
    out_cotangent,
    segment_ids,
    qkv_weight,
    out_weight,
    up_weight,
    down_weight,
    norm_gains,
    bias_rows,
    up_bias,
    qkv_moments,
    out_moments,
    up_moments,
    down_moments,
    gain_moments,
    bias_moments,
    up_bias_moments,
):
    mp = lax.axis_size("mp")
    me = lax.axis_index("mp")
    dp = lax.axis_size("dp")
    dp_me = lax.axis_index("dp")
    width = qkv_weight.shape[2]
    units = up_weight.shape[1]
    tokens, dim = layer_input.shape
    rows = tokens // mp
    pairs = width // PAIR
    heads_local = width // HEAD_DIM
    low = jnp.bfloat16
    block = min(512, tokens)
    column_start = me * width

    def relative(value, axis):
        shape = value.shape
        value = value.reshape(shape[:axis] + (mp, rows) + shape[axis + 1 :])
        parts = [pick(value, me ^ j, axis) for j in range(mp)]
        return jnp.concatenate(parts, axis=axis)

    qkv_low = qkv_weight.astype(low)
    by_pair = qkv_low.reshape(3, -1, pairs, PAIR).transpose(1, 2, 0, 3).reshape(-1, 3 * width)
    qkv_full = lax.all_gather(by_pair, "dp", axis=0, tiled=True)
    weight_set = jnp.concatenate(
        [up_weight.astype(low), down_weight.astype(low), out_weight.astype(low)], axis=1
    )
    inputs = relative(layer_input, 0)
    input_halves = core_halves(inputs.T)
    ids = relative(segment_ids.reshape(-1), 0)
    document = jnp.arange(PAIR, dtype=jnp.int32)
    same = ids[:, None] == document[None, :]
    key_marks = jnp.where(same | (document[None, :] > 2), 0.0, very_low).astype(low)
    query_marks = same.T.astype(low)
    head_bias = lax.dynamic_slice_in_dim(bias_rows[:2], column_start, width, 1)

    queries, queries_t, key_rows, keys_t, values_all, values_t = project(
        inputs, qkv_full, head_bias, key_marks
    )
    weight_set = after(weight_set, qkv_full, key_marks, query_marks, *input_halves)
    weights_all = lax.all_gather(weight_set, ("mp", "dp"), axis=0, tiled=True)
    weights_all = weights_all.reshape(mp, dim, -1)
    qkv_all = lax.all_gather(after(qkv_full, weights_all), "mp", axis=0, tiled=False)
    own_core = (dp_me & 1).astype(jnp.int32).reshape(1)

    calls = [(0, pairs - 1), (pairs - 1, 1)] if pairs > 1 else [(0, 1)]
    place = [(call, at) for call, (_, count) in enumerate(calls) for at in range(count)]
    saved, attended_rel, tops = [], [[] for _ in range(mp)], []
    for first, count in calls:
        probs, attended_t, attended, totals, maxima = attention_forward(
            key_rows, queries_t, query_marks, values_t, first, count, block
        )
        saved.append((probs, attended_t, totals))
        tops.append(maxima)
        for j in range(mp):
            piece = attended[j * rows : (j + 1) * rows]
            attended_rel[j].append(piece if j == 0 else swap(piece, "mp", j))
    head_max = jnp.max(jnp.concatenate(tops).reshape(heads_local, PAIR), axis=1)
    head_max = head_max * HEAD_DIM ** (-0.5)
    attended_all = jnp.concatenate([piece for parts in attended_rel for piece in parts], axis=1)

    out_rel = [pick(weights_all[:, :, 2 * units :], me ^ j, 0) for j in range(mp)]
    branch = times_transposed(attended_all, jnp.concatenate(out_rel, axis=1))
    summed = inputs[:rows].astype(jnp.float32) + branch + bias_rows[2]
    normed, first_norm_pull = jax.vjp(norm_rows, summed, norm_gains[0], bias_rows[4])
    normed_low = normed.astype(low)
    hidden_low, slope, ffn_out = feed_forward(
        normed_low, weights_all, up_bias[None], units
    )
    total = normed + ffn_out + bias_rows[3]
    result, second_norm_pull = jax.vjp(norm_rows, total, norm_gains[1], bias_rows[5])
    total_grad, second_gain_grad, second_shift_grad = second_norm_pull(
        out_cotangent.astype(jnp.float32)
    )
    total_low = total_grad.astype(low)
    total_low = after(total_low, qkv_all)
    up_bias_grad, feed_grad, sent, own = feed_back(
        own_core, dp, total_low, normed_low, weights_all, slope, hidden_low, units
    )
    feed_low = (own + swap(sent, "dp", 1).astype(jnp.float32)).astype(low)
    summed_grad, first_gain_grad, first_shift_grad = first_norm_pull(feed_grad + total_grad)
    summed_low = summed_grad.astype(low)
    grad_rel = [[None] * mp for _ in range(pairs)]
    for j in reversed(range(mp)):
        piece = jnp.dot(summed_low, out_rel[j], preferred_element_type=jnp.float32).astype(low)
        for pair in range(pairs):
            part = piece[:, pair * PAIR : (pair + 1) * PAIR]
            if j and pair:
                part = after(part, grad_rel[0][j])
            grad_rel[pair][j] = part if j == 0 else swap(part, "mp", j)
        summed_late = after(summed_low, piece) if j == mp - 1 else summed_late
    feed_part = over_chips(feed_low.reshape(-1, mp * units))
    out_part = core_first(core_halves(summed_late.T), attended_all)

    slot = lax.broadcasted_iota(jnp.int32, (dp * mp, heads_local), 0)
    slots = jnp.where(slot == dp_me * mp + me, head_max[None], 0.0)
    early = jnp.concatenate(
        [
            first_gain_grad,
            second_gain_grad,
            jnp.sum(summed_grad, axis=0),
            jnp.sum(total_grad, axis=0),
            first_shift_grad,
            second_shift_grad,
            up_bias_grad.reshape(-1),
            slots.reshape(-1),
        ]
    )
    waiting = sum_steps()

    def add_step(value, *others):
        name, mask = waiting.pop(0)
        value = after(value, *others)
        return value + swap(value, name, mask)

    early = add_step(early)
    halves_other, halves_own = input_halves
    own_rows, got_rows = [], [[] for _ in range(mp - 1)]
    sent_pieces, qkv_pieces, bias_pieces = [], [], []
    chains, chained = [], 0

    def own_piece(pair, *others):
        grads, got = sent_pieces[pair]
        own_part = jnp.dot(after(halves_own, *others), grads, preferred_element_type=jnp.float32)
        return own_part + got.astype(jnp.float32)

    grads_low = None
    for pair, (call, at) in enumerate(place):
        probs, attended_t, totals = saved[call]
        ready = [feed_low, out_part, early] if pair == 0 else [early, grads_low, *sending]
        if pair > 1:
            ready += [rows_of[pair - 2] for rows_of in got_rows] + [qkv_pieces[pair - 2]]
        if len(qkv_pieces) > chained:
            fresh = qkv_pieces[chained:]
            fresh = [out_part, *fresh] if chained == 0 else fresh
            chains.append((0, by_bits(jnp.concatenate(fresh, axis=1))))
            chained = len(qkv_pieces)
        moving = []
        for step, value in chains:
            if step == chip_steps():
                moving.append((step, value, None))
                continue
            sent, kept = halve_parts(value, "dp", step + 1, chip_steps() - 1 - step)
            sent = after(sent, grads_low)
            ready.append(sent)
            moving.append((step + 1, kept, swap(sent, "dp", 2 << step)))
        grad_parts = list(grad_rel[pair])
        if pair > 0:
            grad_parts[0] = after(grad_parts[0], grads_low)
        grad_now = after(jnp.concatenate(grad_parts, axis=0), *ready)
        if waiting:
            early = add_step(early, *([] if grads_low is None else [grads_low]))
        grads_low, head_sums = attention_backward(
            probs, grad_now, attended_t, totals, queries, values_all, keys_t, pair, at
        )
        bias_pieces.append(head_sums)
        if pair > 0:
            qkv_pieces.append(own_piece(pair - 1, grads_low))
        chains = [
            (step, kept if got is None else after(kept, grads_low) + got.astype(jnp.float32))
            for step, kept, got in moving
        ]
        own_rows.append(grads_low[:rows])
        sending = [grads_low[j * rows : (j + 1) * rows] for j in range(1, mp)]
        for j in range(1, mp):
            got_rows[j - 1].append(swap(sending[j - 1], "mp", j))
        sent = jnp.dot(halves_other, grads_low, preferred_element_type=jnp.float32).astype(low)
        sent_pieces.append((grads_low, swap(sent, "dp", 1)))
        sending.append(sent)
    qkv_pieces.append(own_piece(pairs - 1))
    while waiting:
        early = add_step(early)
    parts = feed_part.astype(jnp.float32).reshape(2, -1, mp, units)
    up_sum, down_sum = over_mp(parts[0]), over_mp(parts[1])
    gain_sum = early[: 2 * dim].reshape(2, dim)
    late_biases = early[2 * dim : 6 * dim].reshape(4, dim)
    unit_sum = early[6 * dim : 6 * dim + units * mp]
    group_max = jnp.max(early[6 * dim + units * mp :].reshape(dp, mp, heads_local), axis=0)
    local_max = pick(group_max, me, 0)

    input_grad = summed_grad + times_transposed(
        jnp.concatenate(own_rows, axis=1), qkv_full
    )
    last_parts = []
    for j in range(1, mp):
        others = pick(qkv_all, me ^ j, 0)
        parts = got_rows[j - 1]
        if pairs > 1:
            input_grad = input_grad + times_transposed(
                jnp.concatenate(parts[:-1], axis=1), others[:, : -3 * PAIR]
            )
        last_parts.append((parts[-1], others[:, -3 * PAIR :]))
    most_grad = input_grad
    for got, others in last_parts:
        input_grad = input_grad + times_transposed(got, others)
    fresh = qkv_pieces[chained:]
    fresh = [out_part, *fresh] if chained == 0 else fresh
    summing = by_bits(jnp.concatenate(fresh, axis=1))
    for step in range(chip_steps()):
        while chains and chains[-1][0] == step:
            summing = jnp.concatenate([chains.pop()[1], summing], axis=-1)
        summing = halve(summing, "dp", step + 1, chip_steps() - 1 - step)
        if step == 0:
            summing = after(summing, most_grad)
    summing = jnp.concatenate([value for _, value in chains] + [summing], axis=-1)
    out_sum = summing[:, : mp * width]
    qkv_sum = summing[:, mp * width :].reshape(-1, pairs, 3, PAIR)
    out_sum = over_mp_relative([out_sum[:, j * width : (j + 1) * width] for j in range(mp)])
    qkv_sum = qkv_sum.transpose(2, 0, 1, 3).reshape(3, -1, width)

    head_biases = lax.dynamic_update_slice_in_dim(
        jnp.zeros((2, width * mp), jnp.float32),
        jnp.concatenate(bias_pieces, axis=1),
        column_start,
        1,
    )
    for name, mask in sum_steps():
        head_biases = head_biases + swap(head_biases, name, mask)
    bias_sum = jnp.concatenate([head_biases, late_biases], axis=0)

    grad_scale = lax.rsqrt(jnp.float32(tokens * dp))
    step_value = jnp.float32(ADAM_STEP)
    new_qkv, next_qkv = adam_update(qkv_weight, qkv_moments, qkv_sum * grad_scale, step_value)
    new_out, next_out = adam_update(out_weight, out_moments, out_sum * grad_scale, step_value)
    new_up, next_up = adam_update(up_weight, up_moments, up_sum * grad_scale, step_value)
    new_down, next_down = adam_update(down_weight, down_moments, down_sum * grad_scale, step_value)
    new_gains, next_gains = adam_update(norm_gains, gain_moments, gain_sum * grad_scale, step_value)
    new_biases, next_biases = adam_update(
        bias_rows, bias_moments, bias_sum * grad_scale, step_value
    )
    new_up_bias, next_up_bias = adam_update(
        up_bias, up_bias_moments, unit_sum * grad_scale, step_value
    )
    factor = jnp.sqrt(clip_tau / jnp.maximum(local_max, clip_tau))
    column = jnp.repeat(factor, HEAD_DIM)
    scales = jnp.stack([column, column, jnp.ones_like(column)])[:, None, :]
    new_qkv = new_qkv * scales
    return (
        result.astype(jnp.bfloat16),
        input_grad,
        new_qkv,
        new_out,
        new_up,
        new_down,
        new_gains,
        new_biases,
        new_up_bias,
        next_qkv,
        next_out,
        next_up,
        next_down,
        next_gains,
        next_biases,
        next_up_bias,
    )


def solution(mesh):
    placed = (
        P("dp", None),
        P(("dp", "mp"), None),
        P("dp", None),
        P(None, "dp", "mp"),
        P("dp", "mp"),
        P("dp", "mp"),
        P("dp", "mp"),
        P(),
        P(),
        P(),
        P(None, None, "dp", "mp"),
        P(None, "dp", "mp"),
        P(None, "dp", "mp"),
        P(None, "dp", "mp"),
        P(),
        P(),
        P(),
    )
    return jax.shard_map(
        body,
        mesh=mesh,
        in_specs=placed,
        out_specs=(
            P(("dp", "mp"), None),
            P(("dp", "mp"), None),
            P(None, "dp", "mp"),
            P("dp", "mp"),
            P("dp", "mp"),
            P("dp", "mp"),
            P(),
            P(),
            P(),
            P(None, None, "dp", "mp"),
            P(None, "dp", "mp"),
            P(None, "dp", "mp"),
            P(None, "dp", "mp"),
            P(),
            P(),
            P(),
        ),
        check_vma=False,
    )
```

```python
import functools

import jax
import jax.numpy as jnp
from jax import lax
from jax.experimental import pallas as pl
from jax.experimental.pallas import tpu as pltpu
from jax.sharding import PartitionSpec as P

HEAD_DIM = 64
ADAM_STEP = 5
PAIR = 2 * HEAD_DIM
LOG2E = 1.4426950408889634

low = jnp.bfloat16
f32 = jnp.float32
very_low = -1e30
clip_tau = 5.0
learn_rate = 0.25
weight_decay = 0.1
moment_beta = 0.5
adam_epsilon = 1e-08


def norm_rows(values, gain_row, shift_row):
    center = values - jnp.mean(values, axis=-1, keepdims=True)
    spread = jnp.mean(center * center, axis=-1, keepdims=True)
    return center * lax.rsqrt(spread + 1e-05) * gain_row + shift_row


def times_transposed(left_side, right_side):
    return lax.dot_general(
        left_side, right_side, (((1,), (1,)), ((), ())), preferred_element_type=jnp.float32
    )


def adam_update(param, moments, grad, step_value):
    first_moment = moment_beta * moments[0] + (1.0 - moment_beta) * grad
    second_moment = moment_beta * moments[1] + (1.0 - moment_beta) * grad * grad
    correct = 1.0 - jnp.power(moment_beta, step_value)
    update = first_moment / correct / (jnp.sqrt(second_moment / correct) + adam_epsilon)
    return (
        param - learn_rate * (update + weight_decay * param),
        jnp.stack([first_moment, second_moment]),
    )


def dot(left, right):
    return lax.dot_general(left, right, (((1,), (0,)), ((), ())), preferred_element_type=f32)


def dot_nt(left, right):
    return lax.dot_general(left, right, (((1,), (1,)), ((), ())), preferred_element_type=f32)


def kernel_params(axes=1):
    return pltpu.CompilerParams(
        vmem_limit_bytes=58 * 2**20, dimension_semantics=("arbitrary",) * axes
    )


def brief(flops):
    return pl.CostEstimate(flops=flops // 16, bytes_accessed=2**20, transcendentals=0)


def project_kernel(pairs, x, weights, biases, marks, q_ref, qt_ref, k_ref, kt_ref, v_ref, vt_ref):
    for pair in range(pairs):
        span = slice(pair * PAIR, (pair + 1) * PAIR)
        every = dot(x[...], weights[:, 3 * pair * PAIR : 3 * (pair + 1) * PAIR])
        q = every[:, :PAIR] + biases[0:1, span]
        k = every[:, PAIR : 2 * PAIR]
        v = every[:, 2 * PAIR :] + biases[1:2, span]
        q_ref[:, span] = q.astype(low)
        qt_ref[span, :] = q.T.astype(low)
        k_ref[pair, :, :PAIR] = k.astype(low)
        k_ref[pair, :, PAIR:] = marks[...]
        kt_ref[span, :] = k.T.astype(low)
        v_ref[:, span] = v.astype(low)
        vt_ref[span, :] = v.T.astype(low)


def project(x, weights, biases, marks):
    tokens, dim = x.shape
    width = weights.shape[1] // 3
    pairs = width // PAIR
    block = min(512, tokens)
    rows = lambda n: pl.BlockSpec((block, n), lambda i: (i, 0))
    columns = pl.BlockSpec((width, block), lambda i: (0, i))
    natural = jax.ShapeDtypeStruct((tokens, width), low)
    turned = jax.ShapeDtypeStruct((width, tokens), low)
    return pl.pallas_call(
        functools.partial(project_kernel, pairs),
        grid=(tokens // block,),
        in_specs=[
            rows(dim),
            pl.BlockSpec((dim, 3 * width), lambda i: (0, 0)),
            pl.BlockSpec((2, width), lambda i: (0, 0)),
            rows(PAIR),
        ],
        out_specs=[
            rows(width),
            columns,
            pl.BlockSpec((pairs, block, 2 * PAIR), lambda i: (0, i, 0)),
            columns,
            rows(width),
            columns,
        ],
        out_shape=[
            natural,
            turned,
            jax.ShapeDtypeStruct((pairs, tokens, 2 * PAIR), low),
            turned,
            natural,
            turned,
        ],
        compiler_params=kernel_params(),
        cost_estimate=brief(6 * tokens * dim * width),
        name="project",
    )(x, weights, biases, marks)


def forward_kernel(
    bq, ch, tokens, k_cur, k_nxt, q_cur, q_nxt, s_cur, s_nxt, vt,
    p_ref, ot_ref, o_ref, l_ref, m_ref, score_a, score_b, max_a, max_b,
):
    zeros = jnp.zeros((HEAD_DIM, bq), low)
    factor = f32(LOG2E * HEAD_DIM**-0.5)
    steps = tokens // ch
    nq = tokens // bq

    def query_rows(q_ref, marks, head):
        q = q_ref[head * HEAD_DIM : (head + 1) * HEAD_DIM, :]
        parts = [q, zeros] if head == 0 else [zeros, q]
        return jnp.concatenate(parts + [marks[...]], axis=0)

    def scores(keys, q, out, step, top):
        part = dot(keys[step * ch : (step + 1) * ch, :], q)
        out[step * ch : (step + 1) * ch, :] = part
        return jnp.maximum(top, jnp.max(part.reshape(ch // 8, 8, bq), axis=0))

    def finish(top, out):
        out[...] = jnp.broadcast_to(jnp.max(top, axis=0, keepdims=True), (8, bq))

    lowest = jnp.full((8, bq), -3e38, f32)

    @pl.when(pl.program_id(0) == 0)
    def _():
        q = query_rows(q_cur, s_cur, 0)
        top = lowest
        for step in range(steps):
            top = scores(k_cur, q, score_a, step, top)
        finish(top, max_a)

    def phase(head, s_in, m_in, keys, q, s_out, m_out):
        top_row = m_in[0:1, :]
        top = lowest
        sums = jnp.zeros((8, bq), f32)
        total = jnp.zeros((HEAD_DIM, bq), f32)
        for step in range(steps):
            span = slice(step * ch, (step + 1) * ch)
            top = scores(keys, q, s_out, step, top)
            p = jnp.exp2((s_in[span, :] - top_row) * factor)
            sums = sums + jnp.sum(p.reshape(ch // 8, 8, bq), axis=0)
            p_low = p.astype(low)
            p_ref[0, head, 0, span, :] = p_low
            total = total + dot(vt[head * HEAD_DIM : (head + 1) * HEAD_DIM, span], p_low)
        finish(top, m_out)
        row_sum = jnp.sum(sums, axis=0, keepdims=True)
        l_ref[0, head : head + 1, :] = row_sum
        best = top_row[:, :PAIR]
        for first in range(PAIR, bq, PAIR):
            best = jnp.maximum(best, top_row[:, first : first + PAIR])
        here = jnp.where(pl.program_id(0) % nq == 0, lowest[0:1, :PAIR], m_ref[0, head : head + 1, :])
        m_ref[0, head : head + 1, :] = jnp.maximum(here, best)
        return total / row_sum

    first = phase(0, score_a, max_a, k_cur, query_rows(q_cur, s_cur, 1), score_b, max_b)
    second = phase(1, score_b, max_b, k_nxt, query_rows(q_nxt, s_nxt, 0), score_a, max_a)
    both = jnp.concatenate([first, second], axis=0)
    ot_ref[...] = both
    o_ref[...] = both.T.astype(low)


def attention_forward(keys, q_t, marks_t, v_t, first, pairs, bq, ch=512):
    _, tokens, _ = keys.shape
    nq = tokens // bq
    ch = min(ch, tokens)
    count = pairs * nq
    now = lambda i: i
    later = lambda i: jnp.minimum(i + 1, count - 1)
    key_spec = lambda at: pl.BlockSpec(
        (None, tokens, 2 * PAIR), lambda i: (first + at(i) // nq, 0, 0)
    )
    query_spec = lambda at: pl.BlockSpec((PAIR, bq), lambda i: (first + at(i) // nq, at(i) % nq))
    mark_spec = lambda at: pl.BlockSpec((PAIR, bq), lambda i: (0, at(i) % nq))
    row_spec = pl.BlockSpec((1, 2, bq), lambda i: (i // nq, 0, i % nq))
    size = 2 * pairs * tokens * tokens
    return pl.pallas_call(
        functools.partial(forward_kernel, bq, ch, tokens),
        grid=(count,),
        in_specs=[
            key_spec(now), key_spec(later), query_spec(now), query_spec(later),
            mark_spec(now), mark_spec(later),
            pl.BlockSpec((PAIR, tokens), lambda i: (first + i // nq, 0)),
        ],
        out_specs=[
            pl.BlockSpec((1, 2, 1, tokens, bq), lambda i: (i // nq, 0, i % nq, 0, 0)),
            pl.BlockSpec((PAIR, bq), lambda i: (i // nq, i % nq)),
            pl.BlockSpec((bq, PAIR), lambda i: (i % nq, i // nq)),
            row_spec,
            pl.BlockSpec((1, 2, PAIR), lambda i: (i // nq, 0, 0)),
        ],
        out_shape=[
            jax.ShapeDtypeStruct((pairs, 2, nq, tokens, bq), low),
            jax.ShapeDtypeStruct((pairs * PAIR, tokens), f32),
            jax.ShapeDtypeStruct((tokens, pairs * PAIR), low),
            jax.ShapeDtypeStruct((pairs, 2, tokens), f32),
            jax.ShapeDtypeStruct((pairs, 2, PAIR), f32),
        ],
        scratch_shapes=[
            pltpu.VMEM((tokens, bq), f32),
            pltpu.VMEM((tokens, bq), f32),
            pltpu.VMEM((8, bq), f32),
            pltpu.VMEM((8, bq), f32),
        ],
        compiler_params=kernel_params(),
        cost_estimate=brief(16 * HEAD_DIM * size),
        name="attend",
    )(keys, keys, q_t, q_t, marks_t, marks_t, v_t)


def backward_kernel(
    bq, ch, tokens, p_ref, grad, out_t, totals, q, v, kt, g_ref, b_ref, key_acc, value_acc, sums
):
    step_q = pl.program_id(0)

    @pl.when(step_q == 0)
    def _():
        key_acc[...] = jnp.zeros_like(key_acc)
        value_acc[...] = jnp.zeros_like(value_acc)
        sums[...] = jnp.zeros_like(sums)

    zeros = jnp.zeros((HEAD_DIM, bq), low)
    scale = f32(HEAD_DIM**-0.5)
    lane = lax.broadcasted_iota(jnp.int32, (bq, PAIR), 1)

    def diagonal(x):
        zero = jnp.zeros_like(x)
        return jnp.concatenate(
            [jnp.where(lane < HEAD_DIM, x, zero), jnp.where(lane >= HEAD_DIM, x, zero)], axis=0
        )

    grad_t = grad[...].astype(f32).T
    scaled_t, deltas = [], []
    for head in range(2):
        inverse = 1.0 / totals[0, head : head + 1, :]
        span = slice(head * HEAD_DIM, (head + 1) * HEAD_DIM)
        part = grad_t[span] * inverse
        deltas.append(jnp.sum(part * out_t[span, :], axis=0, keepdims=True))
        scaled_t.append(part)
    scaled = jnp.concatenate(scaled_t, axis=0).T.astype(low)
    grad_rows = diagonal(scaled)
    query_rows = diagonal(q[...])
    grad_columns = [
        jnp.concatenate([scaled_t[0].astype(low), zeros], axis=0),
        jnp.concatenate([zeros, scaled_t[1].astype(low)], axis=0),
    ]
    query_grads = [jnp.zeros((HEAD_DIM, bq), f32) for _ in range(2)]
    for step in range(tokens // ch):
        span = slice(step * ch, (step + 1) * ch)
        values = v[span, :]
        probs, score_grads = [], []
        for head in range(2):
            prob_grad = dot(values, grad_columns[head])
            p = p_ref[0, head, 0, span, :]
            score_grad = (p.astype(f32) * (prob_grad - deltas[head])).astype(low)
            probs.append(p)
            score_grads.append(score_grad)
            query_grads[head] = query_grads[head] + dot(
                kt[head * HEAD_DIM : (head + 1) * HEAD_DIM, span], score_grad
            )
        value_acc[span, :] += dot(jnp.concatenate(probs, axis=1), grad_rows)
        key_acc[span, :] += dot(jnp.concatenate(score_grads, axis=1), query_rows)
    query_grad = jnp.concatenate(query_grads, axis=0).T * scale
    g_ref[pl.ds(pl.multiple_of(step_q * bq, bq), bq), 0:PAIR] = query_grad.astype(low)
    sums[...] += jnp.sum(query_grad.reshape(bq // 8, 8, PAIR), axis=0)

    @pl.when(step_q == pl.num_programs(0) - 1)
    def _():
        g_ref[:, PAIR : 2 * PAIR] = (key_acc[...] * scale).astype(low)
        value_grad = value_acc[...]
        g_ref[:, 2 * PAIR :] = value_grad.astype(low)
        b_ref[0:1, :] = jnp.sum(sums[...], axis=0, keepdims=True)
        b_ref[1:2, :] = jnp.sum(value_grad, axis=0, keepdims=True)


def attention_backward(probs, grad, out_t, totals, q, v, k_t, pair, at, ch=1536):
    _, _, nq, tokens, bq = probs.shape
    ch = min(ch, tokens)
    size = 2 * tokens * tokens
    return pl.pallas_call(
        functools.partial(backward_kernel, bq, ch, tokens),
        grid=(nq,),
        in_specs=[
            pl.BlockSpec((1, 2, 1, tokens, bq), lambda i: (at, 0, i, 0, 0)),
            pl.BlockSpec((bq, PAIR), lambda i: (i, 0)),
            pl.BlockSpec((PAIR, bq), lambda i: (at, i)),
            pl.BlockSpec((1, 2, bq), lambda i: (at, 0, i)),
            pl.BlockSpec((bq, PAIR), lambda i: (i, pair)),
            pl.BlockSpec((tokens, PAIR), lambda i: (0, pair)),
            pl.BlockSpec((PAIR, tokens), lambda i: (pair, 0)),
        ],
        out_specs=[
            pl.BlockSpec((tokens, 3 * PAIR), lambda i: (0, 0)),
            pl.BlockSpec((2, PAIR), lambda i: (0, 0)),
        ],
        out_shape=[
            jax.ShapeDtypeStruct((tokens, 3 * PAIR), low),
            jax.ShapeDtypeStruct((2, PAIR), f32),
        ],
        scratch_shapes=[
            pltpu.VMEM((tokens, PAIR), f32),
            pltpu.VMEM((tokens, PAIR), f32),
            pltpu.VMEM((8, PAIR), f32),
        ],
        compiler_params=kernel_params(),
        cost_estimate=brief(32 * HEAD_DIM * size),
        name="attend_back",
    )(probs, grad, out_t, totals, q, v, k_t)


def gelu_and_slope(x):
    size = jnp.abs(x) * f32(0.7071067811865476)
    t = 1.0 / (1.0 + f32(0.3275911) * size)
    bell = jnp.exp2(x * x * f32(-0.5 * LOG2E))
    poly = f32(1.061405429 / 2)
    for coefficient in (-1.453152027, 1.421413741, -0.284496736, 0.254829592):
        poly = poly * t + f32(coefficient / 2)
    tail = poly * t * bell
    phi = jnp.where(x >= 0, 1.0 - tail, tail)
    return x * phi, phi + x * bell * f32(0.3989422804014327)


def feed_kernel(rows, ch, x, up, down, bias, hidden_ref, slope_ref, out_ref):
    @pl.when(pl.program_id(0) == 0)
    def _():
        out_ref[...] = jnp.zeros_like(out_ref)

    def finish(span, pre):
        hidden, slope = gelu_and_slope(pre + bias[...])
        hidden = hidden.astype(low)
        hidden_ref[span, :] = hidden
        slope_ref[span, :] = slope.astype(low)
        out_ref[span, :] += dot_nt(hidden, down[...])

    before = None
    for first in range(0, rows, ch):
        span = slice(first, first + ch)
        pre = dot(x[span, :], up[...])
        if before is not None:
            finish(*before)
        before = (span, pre)
    finish(*before)


def feed_forward(x, weights, bias, units, block=1024, ch=512):
    rows, dim = x.shape
    groups = weights.shape[0]
    block = min(block, units)
    per = units // block
    ch = ch if rows % ch == 0 else rows
    every = groups * units
    weight = lambda skip: pl.BlockSpec(
        (None, dim, block), lambda i: (i // per, 0, skip * per + i % per)
    )
    part = pl.BlockSpec((rows, block), lambda i: (0, i))
    whole = pl.BlockSpec((rows, dim), lambda i: (0, 0))
    return pl.pallas_call(
        functools.partial(feed_kernel, rows, ch),
        grid=(groups * per,),
        in_specs=[whole, weight(0), weight(1), pl.BlockSpec((1, block), lambda i: (0, i))],
        out_specs=[part, part, whole],
        out_shape=[
            jax.ShapeDtypeStruct((rows, every), low),
            jax.ShapeDtypeStruct((rows, every), low),
            jax.ShapeDtypeStruct((rows, dim), f32),
        ],
        compiler_params=kernel_params(),
        cost_estimate=brief(4 * rows * dim * every),
        name="feed",
    )(x, weights, weights, bias)


def feed_back_kernel(
    rows, ch, blocks, core, x, normed, up, down, slope, hidden,
    sum_ref, out_ref, sent_ref, own_ref, x_t, normed_t, pre_all,
):
    half = x_t.shape[0] // 2
    size = 2 * half // blocks

    @pl.when(pl.program_id(0) == 0)
    def _():
        out_ref[...] = jnp.zeros_like(out_ref)
        for source, turned in ((x, x_t), (normed, normed_t)):
            for first in range(0, blocks, 2):
                pair = source[:, first * size : (first + 2) * size].T
                for odd in range(2):
                    own = jnp.where(core[0] == odd, half, 0)
                    at = pl.multiple_of(own + first // 2 * size, size)
                    turned[pl.ds(at, size), :] = pair[odd * size : (odd + 1) * size]

    block = slope.shape[1]
    sums = jnp.zeros((8, block), f32)

    def finish(span, hidden_grad, sums):
        pre = hidden_grad * slope[span, :].astype(f32)
        sums = sums + jnp.sum(pre.reshape(ch // 8, 8, block), axis=0)
        pre = pre.astype(low)
        pre_all[span, :] = pre
        out_ref[span, :] += dot_nt(pre, up[...])
        return sums

    before = None
    for first in range(0, rows, ch):
        span = slice(first, first + ch)
        hidden_grad = dot(x[span, :], down[...])
        if before is not None:
            sums = finish(*before, sums)
        before = (span, hidden_grad)
    owners = (blocks // 2, size, block)
    sent_ref[:, 1] = dot(x_t[:half, :], hidden[...]).astype(low).reshape(owners)
    sums = finish(*before, sums)
    sum_ref[...] = jnp.sum(sums, axis=0, keepdims=True)
    own_ref[:, 1] = dot(x_t[half:, :], hidden[...]).reshape(owners)
    sent_ref[:, 0] = dot(normed_t[:half, :], pre_all[...]).astype(low).reshape(owners)
    own_ref[:, 0] = dot(normed_t[half:, :], pre_all[...]).reshape(owners)


def feed_back(core, blocks, x, normed, weights, slope, hidden, units, block=512, ch=512):
    rows, dim = x.shape
    groups = weights.shape[0]
    block = min(block, units)
    per = units // block
    ch = ch if rows % ch == 0 else rows
    every = groups * units
    weight = lambda skip: pl.BlockSpec(
        (None, dim, block), lambda i: (i // per, 0, skip * per + i % per)
    )
    part = pl.BlockSpec((rows, block), lambda i: (0, i))
    owners = (blocks // 2, 2, dim // blocks)
    half = pl.BlockSpec((None, *owners, block), lambda i: (i // per, 0, 0, 0, i % per))
    once = pl.BlockSpec((rows, dim), lambda i: (0, 0), pipeline_mode=pl.Buffered(1))
    return pl.pallas_call(
        functools.partial(feed_back_kernel, rows, ch, blocks),
        grid=(groups * per,),
        in_specs=[
            pl.BlockSpec(memory_space=pltpu.SMEM), once, once, weight(0), weight(1), part, part
        ],
        out_specs=[
            pl.BlockSpec((1, block), lambda i: (0, i)),
            pl.BlockSpec((rows, dim), lambda i: (0, 0)),
            half,
            half,
        ],
        out_shape=[
            jax.ShapeDtypeStruct((1, every), f32),
            jax.ShapeDtypeStruct((rows, dim), f32),
            jax.ShapeDtypeStruct((groups, *owners, units), low),
            jax.ShapeDtypeStruct((groups, *owners, units), f32),
        ],
        scratch_shapes=[
            pltpu.VMEM((dim, rows), low),
            pltpu.VMEM((dim, rows), low),
            pltpu.VMEM((rows, block), low),
        ],
        compiler_params=kernel_params(),
        cost_estimate=brief(8 * rows * dim * every),
        name="feed_back",
    )(core, x, normed, weights, weights, slope, hidden)


def bits_of(size):
    return size.bit_length() - 1


def swap(value, axis_name, mask):
    size = lax.axis_size(axis_name)
    return lax.ppermute(value, axis_name, [(i, i ^ mask) for i in range(size)])


def pick(value, index, axis):
    return lax.dynamic_index_in_dim(value, index, axis, keepdims=False)


def after(value, *others):
    return lax.optimization_barrier((value,) + others)[0]


def halve_parts(value, axis_name, bit, axis):
    mine = (lax.axis_index(axis_name) >> bit) & 1
    return pick(value, 1 - mine, axis).astype(jnp.bfloat16), pick(value, mine, axis)


def halve(value, axis_name, bit, axis):
    sent, kept = halve_parts(value, axis_name, bit, axis)
    return kept + swap(sent, axis_name, 1 << bit).astype(jnp.float32)


def chip_steps():
    return bits_of(lax.axis_size("dp")) - 1


def by_bits(value):
    return value.reshape((2,) * chip_steps() + (-1, value.shape[-1]))


def core_halves(rows_t):
    core = lax.axis_index("dp") & 1
    tokens = rows_t.shape[1]
    split = rows_t.reshape(lax.axis_size("dp") // 2, 2, -1, tokens)
    return pick(split, 1 - core, 1).reshape(-1, tokens), pick(split, core, 1).reshape(-1, tokens)


def core_first(halves, right):
    other, own = halves
    sent = jnp.dot(other, right, preferred_element_type=jnp.float32).astype(jnp.bfloat16)
    got = swap(sent, "dp", 1)
    return jnp.dot(own, right, preferred_element_type=jnp.float32) + got.astype(jnp.float32)


def over_chips(value):
    size = lax.axis_size("mp") * lax.axis_size("dp")
    groups = [[i for i in range(size) if i % 2 == core] for core in range(2)]
    return lax.psum_scatter(
        value, ("mp", "dp"), scatter_dimension=0, axis_index_groups=groups, tiled=True
    )


def over_mp_relative(blocks):
    blocks = list(blocks)
    for step in reversed(range(bits_of(len(blocks)))):
        size = 1 << step
        blocks = [
            blocks[j] + swap(blocks[j + size].astype(jnp.bfloat16), "mp", size).astype(jnp.float32)
            for j in range(size)
        ]
    return blocks[0]


def sum_steps():
    return [
        (name, 1 << step) for name in ("mp", "dp") for step in range(bits_of(lax.axis_size(name)))
    ]


def body(
    layer_input,
    out_cotangent,
    segment_ids,
    qkv_weight,
    out_weight,
    up_weight,
    down_weight,
    norm_gains,
    bias_rows,
    up_bias,
    qkv_moments,
    out_moments,
    up_moments,
    down_moments,
    gain_moments,
    bias_moments,
    up_bias_moments,
):
    mp = lax.axis_size("mp")
    me = lax.axis_index("mp")
    dp = lax.axis_size("dp")
    dp_me = lax.axis_index("dp")
    width = qkv_weight.shape[2]
    units = up_weight.shape[1]
    tokens, dim = layer_input.shape
    rows = tokens // mp
    pairs = width // PAIR
    heads_local = width // HEAD_DIM
    low = jnp.bfloat16
    block = min(512, tokens)
    column_start = me * width

    def relative(value, axis):
        shape = value.shape
        value = value.reshape(shape[:axis] + (mp, rows) + shape[axis + 1 :])
        parts = [pick(value, me ^ j, axis) for j in range(mp)]
        return jnp.concatenate(parts, axis=axis)

    qkv_low = qkv_weight.astype(low)
    by_pair = qkv_low.reshape(3, -1, pairs, PAIR).transpose(1, 2, 0, 3).reshape(-1, 3 * width)
    qkv_full = lax.all_gather(by_pair, "dp", axis=0, tiled=True)
    weight_set = jnp.concatenate(
        [up_weight.astype(low), down_weight.astype(low), out_weight.astype(low)], axis=1
    )
    inputs = relative(layer_input, 0)
    input_halves = core_halves(inputs.T)
    ids = relative(segment_ids.reshape(-1), 0)
    document = jnp.arange(PAIR, dtype=jnp.int32)
    same = ids[:, None] == document[None, :]
    key_marks = jnp.where(same | (document[None, :] > 2), 0.0, very_low).astype(low)
    query_marks = same.T.astype(low)
    head_bias = lax.dynamic_slice_in_dim(bias_rows[:2], column_start, width, 1)

    queries, queries_t, key_rows, keys_t, values_all, values_t = project(
        inputs, qkv_full, head_bias, key_marks
    )
    weight_set = after(weight_set, qkv_full, key_marks, query_marks, *input_halves)
    weights_all = lax.all_gather(weight_set, ("mp", "dp"), axis=0, tiled=True)
    weights_all = weights_all.reshape(mp, dim, -1)
    qkv_all = lax.all_gather(after(qkv_full, weights_all), "mp", axis=0, tiled=False)
    own_core = (dp_me & 1).astype(jnp.int32).reshape(1)

    calls = [(0, pairs - 1), (pairs - 1, 1)] if pairs > 1 else [(0, 1)]
    place = [(call, at) for call, (_, count) in enumerate(calls) for at in range(count)]
    saved, attended_rel, tops = [], [[] for _ in range(mp)], []
    for first, count in calls:
        probs, attended_t, attended, totals, maxima = attention_forward(
            key_rows, queries_t, query_marks, values_t, first, count, block
        )
        saved.append((probs, attended_t, totals))
        tops.append(maxima)
        for j in range(mp):
            piece = attended[j * rows : (j + 1) * rows]
            attended_rel[j].append(piece if j == 0 else swap(piece, "mp", j))
    head_max = jnp.max(jnp.concatenate(tops).reshape(heads_local, PAIR), axis=1)
    head_max = head_max * HEAD_DIM ** (-0.5)
    attended_all = jnp.concatenate([piece for parts in attended_rel for piece in parts], axis=1)

    out_rel = [pick(weights_all[:, :, 2 * units :], me ^ j, 0) for j in range(mp)]
    branch = times_transposed(attended_all, jnp.concatenate(out_rel, axis=1))
    summed = inputs[:rows].astype(jnp.float32) + branch + bias_rows[2]
    normed, first_norm_pull = jax.vjp(norm_rows, summed, norm_gains[0], bias_rows[4])
    normed_low = normed.astype(low)
    hidden_low, slope, ffn_out = feed_forward(
        normed_low, weights_all, up_bias[None], units
    )
    total = normed + ffn_out + bias_rows[3]
    result, second_norm_pull = jax.vjp(norm_rows, total, norm_gains[1], bias_rows[5])
    total_grad, second_gain_grad, second_shift_grad = second_norm_pull(
        out_cotangent.astype(jnp.float32)
    )
    total_low = total_grad.astype(low)
    total_low = after(total_low, qkv_all)
    up_bias_grad, feed_grad, sent, own = feed_back(
        own_core, dp, total_low, normed_low, weights_all, slope, hidden_low, units
    )
    feed_low = (own + swap(sent, "dp", 1).astype(jnp.float32)).astype(low)
    summed_grad, first_gain_grad, first_shift_grad = first_norm_pull(feed_grad + total_grad)
    summed_low = summed_grad.astype(low)
    grad_rel = [[None] * mp for _ in range(pairs)]
    for j in reversed(range(mp)):
        piece = jnp.dot(summed_low, out_rel[j], preferred_element_type=jnp.float32).astype(low)
        for pair in range(pairs):
            part = piece[:, pair * PAIR : (pair + 1) * PAIR]
            if j and pair:
                part = after(part, grad_rel[0][j])
            grad_rel[pair][j] = part if j == 0 else swap(part, "mp", j)
        summed_late = after(summed_low, piece) if j == mp - 1 else summed_late
    feed_part = over_chips(feed_low.reshape(-1, units))
    out_part = core_first(core_halves(summed_late.T), attended_all)

    slot = lax.broadcasted_iota(jnp.int32, (dp * mp, heads_local), 0)
    slots = jnp.where(slot == dp_me * mp + me, head_max[None], 0.0)
    early = jnp.concatenate(
        [
            first_gain_grad,
            second_gain_grad,
            jnp.sum(summed_grad, axis=0),
            jnp.sum(total_grad, axis=0),
            first_shift_grad,
            second_shift_grad,
            up_bias_grad.reshape(-1),
            slots.reshape(-1),
        ]
    )
    waiting = sum_steps()

    def add_step(value, *others):
        name, mask = waiting.pop(0)
        value = after(value, *others)
        return value + swap(value, name, mask)

    early = add_step(early)
    halves_other, halves_own = input_halves
    own_rows, got_rows = [], [[] for _ in range(mp - 1)]
    sent_pieces, qkv_pieces, bias_pieces = [], [], []
    chains, chained = [], 0

    def own_piece(pair, *others):
        grads, got = sent_pieces[pair]
        own_part = jnp.dot(after(halves_own, *others), grads, preferred_element_type=jnp.float32)
        return own_part + got.astype(jnp.float32)

    grads_low = None
    for pair, (call, at) in enumerate(place):
        probs, attended_t, totals = saved[call]
        ready = [feed_low, out_part, early] if pair == 0 else [early, grads_low, *sending]
        if pair > 1:
            ready += [rows_of[pair - 2] for rows_of in got_rows] + [qkv_pieces[pair - 2]]
        if len(qkv_pieces) > chained:
            fresh = qkv_pieces[chained:]
            fresh = [out_part, *fresh] if chained == 0 else fresh
            chains.append((0, by_bits(jnp.concatenate(fresh, axis=1))))
            chained = len(qkv_pieces)
        moving = []
        for step, value in chains:
            if step == chip_steps():
                moving.append((step, value, None))
                continue
            sent, kept = halve_parts(value, "dp", step + 1, chip_steps() - 1 - step)
            sent = after(sent, grads_low)
            ready.append(sent)
            moving.append((step + 1, kept, swap(sent, "dp", 2 << step)))
        grad_parts = list(grad_rel[pair])
        if pair > 0:
            grad_parts[0] = after(grad_parts[0], grads_low)
        grad_now = after(jnp.concatenate(grad_parts, axis=0), *ready)
        if waiting:
            early = add_step(early, *([] if grads_low is None else [grads_low]))
        grads_low, head_sums = attention_backward(
            probs, grad_now, attended_t, totals, queries, values_all, keys_t, pair, at
        )
        if pair == pairs - 1 and pair > 0:
            kept = [rows_of[pair - 1] for rows_of in got_rows]
            grads_low, head_sums = lax.optimization_barrier((grads_low, head_sums, *kept))[:2]
        bias_pieces.append(head_sums)
        if pair > 0:
            qkv_pieces.append(own_piece(pair - 1, grads_low))
        chains = [
            (step, kept if got is None else after(kept, grads_low) + got.astype(jnp.float32))
            for step, kept, got in moving
        ]
        own_rows.append(grads_low[:rows])
        sending = [grads_low[j * rows : (j + 1) * rows] for j in range(1, mp)]
        for j in range(1, mp):
            got_rows[j - 1].append(swap(sending[j - 1], "mp", j))
        sent = jnp.dot(halves_other, grads_low, preferred_element_type=jnp.float32).astype(low)
        sent_pieces.append((grads_low, swap(sent, "dp", 1)))
        sending.append(sent)
    qkv_pieces.append(own_piece(pairs - 1))
    while waiting:
        early = add_step(early)
    feed_rows = feed_part.shape[0] // 2
    up_sum = feed_part[:feed_rows].astype(jnp.float32)
    down_sum = feed_part[feed_rows:].astype(jnp.float32)
    gain_sum = early[: 2 * dim].reshape(2, dim)
    late_biases = early[2 * dim : 6 * dim].reshape(4, dim)
    unit_sum = early[6 * dim : 6 * dim + units * mp]
    group_max = jnp.max(early[6 * dim + units * mp :].reshape(dp, mp, heads_local), axis=0)
    local_max = pick(group_max, me, 0)

    input_grad = summed_grad + times_transposed(
        jnp.concatenate(own_rows, axis=1), qkv_full
    )
    last_parts = []
    for j in range(1, mp):
        others = pick(qkv_all, me ^ j, 0)
        parts = got_rows[j - 1]
        if pairs > 1:
            input_grad = input_grad + times_transposed(
                jnp.concatenate(parts[:-1], axis=1), others[:, : -3 * PAIR]
            )
        last_parts.append((parts[-1], others[:, -3 * PAIR :]))
    most_grad = input_grad
    for got, others in last_parts:
        input_grad = input_grad + times_transposed(got, others)
    fresh = qkv_pieces[chained:]
    fresh = [out_part, *fresh] if chained == 0 else fresh
    summing = by_bits(jnp.concatenate(fresh, axis=1))
    for step in range(chip_steps()):
        while chains and chains[-1][0] == step:
            summing = jnp.concatenate([chains.pop()[1], summing], axis=-1)
        summing = halve(summing, "dp", step + 1, chip_steps() - 1 - step)
        if step == 0:
            summing = after(summing, most_grad)
    summing = jnp.concatenate([value for _, value in chains] + [summing], axis=-1)
    out_sum = summing[:, : mp * width]
    qkv_sum = summing[:, mp * width :].reshape(-1, pairs, 3, PAIR)
    out_sum = over_mp_relative([out_sum[:, j * width : (j + 1) * width] for j in range(mp)])
    qkv_sum = qkv_sum.transpose(2, 0, 1, 3).reshape(3, -1, width)

    head_biases = lax.dynamic_update_slice_in_dim(
        jnp.zeros((2, width * mp), jnp.float32),
        jnp.concatenate(bias_pieces, axis=1),
        column_start,
        1,
    )
    for name, mask in sum_steps():
        head_biases = head_biases + swap(head_biases, name, mask)
    bias_sum = jnp.concatenate([head_biases, late_biases], axis=0)

    grad_scale = lax.rsqrt(jnp.float32(tokens * dp))
    step_value = jnp.float32(ADAM_STEP)
    new_qkv, next_qkv = adam_update(qkv_weight, qkv_moments, qkv_sum * grad_scale, step_value)
    new_out, next_out = adam_update(out_weight, out_moments, out_sum * grad_scale, step_value)
    new_up, next_up = adam_update(up_weight, up_moments, up_sum * grad_scale, step_value)
    new_down, next_down = adam_update(down_weight, down_moments, down_sum * grad_scale, step_value)
    new_gains, next_gains = adam_update(norm_gains, gain_moments, gain_sum * grad_scale, step_value)
    new_biases, next_biases = adam_update(
        bias_rows, bias_moments, bias_sum * grad_scale, step_value
    )
    new_up_bias, next_up_bias = adam_update(
        up_bias, up_bias_moments, unit_sum * grad_scale, step_value
    )
    factor = jnp.sqrt(clip_tau / jnp.maximum(local_max, clip_tau))
    column = jnp.repeat(factor, HEAD_DIM)
    scales = jnp.stack([column, column, jnp.ones_like(column)])[:, None, :]
    new_qkv = new_qkv * scales
    return (
        result.astype(jnp.bfloat16),
        input_grad,
        new_qkv,
        new_out,
        new_up,
        new_down,
        new_gains,
        new_biases,
        new_up_bias,
        next_qkv,
        next_out,
        next_up,
        next_down,
        next_gains,
        next_biases,
        next_up_bias,
    )


def solution(mesh):
    placed = (
        P("dp", None),
        P(("dp", "mp"), None),
        P("dp", None),
        P(None, "dp", "mp"),
        P("dp", "mp"),
        P("dp", "mp"),
        P("dp", "mp"),
        P(),
        P(),
        P(),
        P(None, None, "dp", "mp"),
        P(None, "dp", "mp"),
        P(None, "dp", "mp"),
        P(None, "dp", "mp"),
        P(),
        P(),
        P(),
    )
    return jax.shard_map(
        body,
        mesh=mesh,
        in_specs=placed,
        out_specs=(
            P(("dp", "mp"), None),
            P(("dp", "mp"), None),
            P(None, "dp", "mp"),
            P("dp", "mp"),
            P("dp", "mp"),
            P("dp", "mp"),
            P(),
            P(),
            P(),
            P(None, None, "dp", "mp"),
            P(None, "dp", "mp"),
            P(None, "dp", "mp"),
            P(None, "dp", "mp"),
            P(),
            P(),
            P(),
        ),
        check_vma=False,
    )
```

```python
import functools

import jax
import jax.numpy as jnp
from jax import lax
from jax.experimental import pallas as pl
from jax.experimental.pallas import tpu as pltpu
from jax.sharding import PartitionSpec as P

HEAD_DIM = 64
ADAM_STEP = 5
PAIR = 2 * HEAD_DIM
LOG2E = 1.4426950408889634

low = jnp.bfloat16
f32 = jnp.float32
very_low = -1e30
clip_tau = 5.0
learn_rate = 0.25
weight_decay = 0.1
moment_beta = 0.5
adam_epsilon = 1e-08


def norm_rows(values, gain_row, shift_row):
    center = values - jnp.mean(values, axis=-1, keepdims=True)
    spread = jnp.mean(center * center, axis=-1, keepdims=True)
    return center * lax.rsqrt(spread + 1e-05) * gain_row + shift_row


def times_transposed(left_side, right_side):
    return lax.dot_general(
        left_side, right_side, (((1,), (1,)), ((), ())), preferred_element_type=jnp.float32
    )


def adam_update(param, moments, grad, step_value):
    first_moment = moment_beta * moments[0] + (1.0 - moment_beta) * grad
    second_moment = moment_beta * moments[1] + (1.0 - moment_beta) * grad * grad
    correct = 1.0 - jnp.power(moment_beta, step_value)
    update = first_moment / correct / (jnp.sqrt(second_moment / correct) + adam_epsilon)
    return (
        param - learn_rate * (update + weight_decay * param),
        jnp.stack([first_moment, second_moment]),
    )


def dot(left, right):
    return lax.dot_general(left, right, (((1,), (0,)), ((), ())), preferred_element_type=f32)


def dot_nt(left, right):
    return lax.dot_general(left, right, (((1,), (1,)), ((), ())), preferred_element_type=f32)


def kernel_params(axes=1):
    return pltpu.CompilerParams(
        vmem_limit_bytes=58 * 2**20, dimension_semantics=("arbitrary",) * axes
    )


def brief(flops):
    return pl.CostEstimate(flops=flops // 16, bytes_accessed=2**20, transcendentals=0)


def project_kernel(pairs, x, weights, biases, marks, q_ref, qt_ref, k_ref, kt_ref, v_ref, vt_ref):
    for pair in range(pairs):
        span = slice(pair * PAIR, (pair + 1) * PAIR)
        every = dot(x[...], weights[:, 3 * pair * PAIR : 3 * (pair + 1) * PAIR])
        q = every[:, :PAIR] + biases[0:1, span]
        k = every[:, PAIR : 2 * PAIR]
        v = every[:, 2 * PAIR :] + biases[1:2, span]
        q_ref[:, span] = q.astype(low)
        qt_ref[span, :] = q.T.astype(low)
        k_ref[pair, :, :PAIR] = k.astype(low)
        k_ref[pair, :, PAIR:] = marks[...]
        kt_ref[span, :] = k.T.astype(low)
        v_ref[:, span] = v.astype(low)
        vt_ref[span, :] = v.T.astype(low)


def project(x, weights, biases, marks):
    tokens, dim = x.shape
    width = weights.shape[1] // 3
    pairs = width // PAIR
    block = min(512, tokens)
    rows = lambda n: pl.BlockSpec((block, n), lambda i: (i, 0))
    columns = pl.BlockSpec((width, block), lambda i: (0, i))
    natural = jax.ShapeDtypeStruct((tokens, width), low)
    turned = jax.ShapeDtypeStruct((width, tokens), low)
    return pl.pallas_call(
        functools.partial(project_kernel, pairs),
        grid=(tokens // block,),
        in_specs=[
            rows(dim),
            pl.BlockSpec((dim, 3 * width), lambda i: (0, 0)),
            pl.BlockSpec((2, width), lambda i: (0, 0)),
            rows(PAIR),
        ],
        out_specs=[
            rows(width),
            columns,
            pl.BlockSpec((pairs, block, 2 * PAIR), lambda i: (0, i, 0)),
            columns,
            rows(width),
            columns,
        ],
        out_shape=[
            natural,
            turned,
            jax.ShapeDtypeStruct((pairs, tokens, 2 * PAIR), low),
            turned,
            natural,
            turned,
        ],
        compiler_params=kernel_params(),
        cost_estimate=brief(6 * tokens * dim * width),
        name="project",
    )(x, weights, biases, marks)


def forward_kernel(
    bq, ch, tokens, k_cur, k_nxt, q_cur, q_nxt, s_cur, s_nxt, vt,
    p_ref, ot_ref, o_ref, l_ref, m_ref, score_a, score_b, max_a, max_b,
):
    zeros = jnp.zeros((HEAD_DIM, bq), low)
    factor = f32(LOG2E * HEAD_DIM**-0.5)
    steps = tokens // ch
    nq = tokens // bq

    def query_rows(q_ref, marks, head):
        q = q_ref[head * HEAD_DIM : (head + 1) * HEAD_DIM, :]
        parts = [q, zeros] if head == 0 else [zeros, q]
        return jnp.concatenate(parts + [marks[...]], axis=0)

    def scores(keys, q, out, step, top):
        part = dot(keys[step * ch : (step + 1) * ch, :], q)
        out[step * ch : (step + 1) * ch, :] = part
        return jnp.maximum(top, jnp.max(part.reshape(ch // 8, 8, bq), axis=0))

    def finish(top, out):
        out[...] = jnp.broadcast_to(jnp.max(top, axis=0, keepdims=True), (8, bq))

    lowest = jnp.full((8, bq), -3e38, f32)

    @pl.when(pl.program_id(0) == 0)
    def _():
        q = query_rows(q_cur, s_cur, 0)
        top = lowest
        for step in range(steps):
            top = scores(k_cur, q, score_a, step, top)
        finish(top, max_a)

    def phase(head, s_in, m_in, keys, q, s_out, m_out):
        top_row = m_in[0:1, :]
        top = lowest
        sums = jnp.zeros((8, bq), f32)
        total = jnp.zeros((HEAD_DIM, bq), f32)
        for step in range(steps):
            span = slice(step * ch, (step + 1) * ch)
            top = scores(keys, q, s_out, step, top)
            p = jnp.exp2((s_in[span, :] - top_row) * factor)
            sums = sums + jnp.sum(p.reshape(ch // 8, 8, bq), axis=0)
            p_low = p.astype(low)
            p_ref[0, head, 0, span, :] = p_low
            total = total + dot(vt[head * HEAD_DIM : (head + 1) * HEAD_DIM, span], p_low)
        finish(top, m_out)
        row_sum = jnp.sum(sums, axis=0, keepdims=True)
        l_ref[0, head : head + 1, :] = row_sum
        best = top_row[:, :PAIR]
        for first in range(PAIR, bq, PAIR):
            best = jnp.maximum(best, top_row[:, first : first + PAIR])
        here = jnp.where(pl.program_id(0) % nq == 0, lowest[0:1, :PAIR], m_ref[0, head : head + 1, :])
        m_ref[0, head : head + 1, :] = jnp.maximum(here, best)
        return total / row_sum

    first = phase(0, score_a, max_a, k_cur, query_rows(q_cur, s_cur, 1), score_b, max_b)
    second = phase(1, score_b, max_b, k_nxt, query_rows(q_nxt, s_nxt, 0), score_a, max_a)
    both = jnp.concatenate([first, second], axis=0)
    ot_ref[...] = both
    o_ref[...] = both.T.astype(low)


def attention_forward(keys, q_t, marks_t, v_t, first, pairs, bq, ch=512):
    _, tokens, _ = keys.shape
    nq = tokens // bq
    ch = min(ch, tokens)
    count = pairs * nq
    now = lambda i: i
    later = lambda i: jnp.minimum(i + 1, count - 1)
    key_spec = lambda at: pl.BlockSpec(
        (None, tokens, 2 * PAIR), lambda i: (first + at(i) // nq, 0, 0)
    )
    query_spec = lambda at: pl.BlockSpec((PAIR, bq), lambda i: (first + at(i) // nq, at(i) % nq))
    mark_spec = lambda at: pl.BlockSpec((PAIR, bq), lambda i: (0, at(i) % nq))
    row_spec = pl.BlockSpec((1, 2, bq), lambda i: (i // nq, 0, i % nq))
    size = 2 * pairs * tokens * tokens
    return pl.pallas_call(
        functools.partial(forward_kernel, bq, ch, tokens),
        grid=(count,),
        in_specs=[
            key_spec(now), key_spec(later), query_spec(now), query_spec(later),
            mark_spec(now), mark_spec(later),
            pl.BlockSpec((PAIR, tokens), lambda i: (first + i // nq, 0)),
        ],
        out_specs=[
            pl.BlockSpec((1, 2, 1, tokens, bq), lambda i: (i // nq, 0, i % nq, 0, 0)),
            pl.BlockSpec((PAIR, bq), lambda i: (i // nq, i % nq)),
            pl.BlockSpec((bq, PAIR), lambda i: (i % nq, i // nq)),
            row_spec,
            pl.BlockSpec((1, 2, PAIR), lambda i: (i // nq, 0, 0)),
        ],
        out_shape=[
            jax.ShapeDtypeStruct((pairs, 2, nq, tokens, bq), low),
            jax.ShapeDtypeStruct((pairs * PAIR, tokens), f32),
            jax.ShapeDtypeStruct((tokens, pairs * PAIR), low),
            jax.ShapeDtypeStruct((pairs, 2, tokens), f32),
            jax.ShapeDtypeStruct((pairs, 2, PAIR), f32),
        ],
        scratch_shapes=[
            pltpu.VMEM((tokens, bq), f32),
            pltpu.VMEM((tokens, bq), f32),
            pltpu.VMEM((8, bq), f32),
            pltpu.VMEM((8, bq), f32),
        ],
        compiler_params=kernel_params(),
        cost_estimate=brief(16 * HEAD_DIM * size),
        name="attend",
    )(keys, keys, q_t, q_t, marks_t, marks_t, v_t)


def backward_kernel(
    bq, ch, tokens, p_ref, grad, out_t, totals, q, v, kt, g_ref, b_ref, key_acc, value_acc, sums
):
    step_q = pl.program_id(0)

    @pl.when(step_q == 0)
    def _():
        key_acc[...] = jnp.zeros_like(key_acc)
        value_acc[...] = jnp.zeros_like(value_acc)
        sums[...] = jnp.zeros_like(sums)

    zeros = jnp.zeros((HEAD_DIM, bq), low)
    scale = f32(HEAD_DIM**-0.5)
    lane = lax.broadcasted_iota(jnp.int32, (bq, PAIR), 1)

    def diagonal(x):
        zero = jnp.zeros_like(x)
        return jnp.concatenate(
            [jnp.where(lane < HEAD_DIM, x, zero), jnp.where(lane >= HEAD_DIM, x, zero)], axis=0
        )

    grad_t = grad[...].astype(f32).T
    scaled_t, deltas = [], []
    for head in range(2):
        inverse = 1.0 / totals[0, head : head + 1, :]
        span = slice(head * HEAD_DIM, (head + 1) * HEAD_DIM)
        part = grad_t[span] * inverse
        deltas.append(jnp.sum(part * out_t[span, :], axis=0, keepdims=True))
        scaled_t.append(part)
    scaled = jnp.concatenate(scaled_t, axis=0).T.astype(low)
    grad_rows = diagonal(scaled)
    query_rows = diagonal(q[...])
    grad_columns = [
        jnp.concatenate([scaled_t[0].astype(low), zeros], axis=0),
        jnp.concatenate([zeros, scaled_t[1].astype(low)], axis=0),
    ]
    query_grads = [jnp.zeros((HEAD_DIM, bq), f32) for _ in range(2)]
    for step in range(tokens // ch):
        span = slice(step * ch, (step + 1) * ch)
        values = v[span, :]
        probs, score_grads = [], []
        for head in range(2):
            prob_grad = dot(values, grad_columns[head])
            p = p_ref[0, head, 0, span, :]
            score_grad = (p.astype(f32) * (prob_grad - deltas[head])).astype(low)
            probs.append(p)
            score_grads.append(score_grad)
            query_grads[head] = query_grads[head] + dot(
                kt[head * HEAD_DIM : (head + 1) * HEAD_DIM, span], score_grad
            )
        value_acc[span, :] += dot(jnp.concatenate(probs, axis=1), grad_rows)
        key_acc[span, :] += dot(jnp.concatenate(score_grads, axis=1), query_rows)
    query_grad = jnp.concatenate(query_grads, axis=0).T * scale
    g_ref[pl.ds(pl.multiple_of(step_q * bq, bq), bq), 0:PAIR] = query_grad.astype(low)
    sums[...] += jnp.sum(query_grad.reshape(bq // 8, 8, PAIR), axis=0)

    @pl.when(step_q == pl.num_programs(0) - 1)
    def _():
        g_ref[:, PAIR : 2 * PAIR] = (key_acc[...] * scale).astype(low)
        value_grad = value_acc[...]
        g_ref[:, 2 * PAIR :] = value_grad.astype(low)
        b_ref[0:1, :] = jnp.sum(sums[...], axis=0, keepdims=True)
        b_ref[1:2, :] = jnp.sum(value_grad, axis=0, keepdims=True)


def attention_backward(probs, grad, out_t, totals, q, v, k_t, pair, at, ch=1536):
    _, _, nq, tokens, bq = probs.shape
    ch = min(ch, tokens)
    size = 2 * tokens * tokens
    return pl.pallas_call(
        functools.partial(backward_kernel, bq, ch, tokens),
        grid=(nq,),
        in_specs=[
            pl.BlockSpec((1, 2, 1, tokens, bq), lambda i: (at, 0, i, 0, 0)),
            pl.BlockSpec((bq, PAIR), lambda i: (i, 0)),
            pl.BlockSpec((PAIR, bq), lambda i: (at, i)),
            pl.BlockSpec((1, 2, bq), lambda i: (at, 0, i)),
            pl.BlockSpec((bq, PAIR), lambda i: (i, pair)),
            pl.BlockSpec((tokens, PAIR), lambda i: (0, pair)),
            pl.BlockSpec((PAIR, tokens), lambda i: (pair, 0)),
        ],
        out_specs=[
            pl.BlockSpec((tokens, 3 * PAIR), lambda i: (0, 0)),
            pl.BlockSpec((2, PAIR), lambda i: (0, 0)),
        ],
        out_shape=[
            jax.ShapeDtypeStruct((tokens, 3 * PAIR), low),
            jax.ShapeDtypeStruct((2, PAIR), f32),
        ],
        scratch_shapes=[
            pltpu.VMEM((tokens, PAIR), f32),
            pltpu.VMEM((tokens, PAIR), f32),
            pltpu.VMEM((8, PAIR), f32),
        ],
        compiler_params=kernel_params(),
        cost_estimate=brief(32 * HEAD_DIM * size),
        name="attend_back",
    )(probs, grad, out_t, totals, q, v, k_t)


def gelu_and_slope(x):
    size = jnp.abs(x) * f32(0.7071067811865476)
    t = 1.0 / (1.0 + f32(0.3275911) * size)
    bell = jnp.exp2(x * x * f32(-0.5 * LOG2E))
    poly = f32(1.061405429 / 2)
    for coefficient in (-1.453152027, 1.421413741, -0.284496736, 0.254829592):
        poly = poly * t + f32(coefficient / 2)
    tail = poly * t * bell
    phi = jnp.where(x >= 0, 1.0 - tail, tail)
    return x * phi, phi + x * bell * f32(0.3989422804014327)


def feed_kernel(rows, ch, x, up, down, bias, hidden_ref, slope_ref, out_ref):
    @pl.when(pl.program_id(0) == 0)
    def _():
        out_ref[...] = jnp.zeros_like(out_ref)

    def finish(span, pre):
        hidden, slope = gelu_and_slope(pre + bias[...])
        hidden = hidden.astype(low)
        hidden_ref[span, :] = hidden
        slope_ref[span, :] = slope.astype(low)
        out_ref[span, :] += dot_nt(hidden, down[...])

    before = None
    for first in range(0, rows, ch):
        span = slice(first, first + ch)
        pre = dot(x[span, :], up[...])
        if before is not None:
            finish(*before)
        before = (span, pre)
    finish(*before)


def feed_forward(x, weights, bias, units, block=1024, ch=512):
    rows, dim = x.shape
    groups = weights.shape[0]
    block = min(block, units)
    per = units // block
    ch = ch if rows % ch == 0 else rows
    every = groups * units
    weight = lambda skip: pl.BlockSpec(
        (None, dim, block), lambda i: (i // per, 0, skip * per + i % per)
    )
    part = pl.BlockSpec((rows, block), lambda i: (0, i))
    whole = pl.BlockSpec((rows, dim), lambda i: (0, 0))
    return pl.pallas_call(
        functools.partial(feed_kernel, rows, ch),
        grid=(groups * per,),
        in_specs=[whole, weight(0), weight(1), pl.BlockSpec((1, block), lambda i: (0, i))],
        out_specs=[part, part, whole],
        out_shape=[
            jax.ShapeDtypeStruct((rows, every), low),
            jax.ShapeDtypeStruct((rows, every), low),
            jax.ShapeDtypeStruct((rows, dim), f32),
        ],
        compiler_params=kernel_params(),
        cost_estimate=pl.CostEstimate(
            flops=4 * rows * dim * every, bytes_accessed=8 * dim * every, transcendentals=0
        ),
        name="feed",
    )(x, weights, weights, bias)


def norm_parts(values):
    center = values - jnp.mean(values, axis=-1, keepdims=True)
    scale = lax.rsqrt(jnp.mean(center * center, axis=-1, keepdims=True) + 1e-05)
    return center * scale, scale


def norm_pull(normal, scale, gain, cotangent):
    grad = cotangent * gain
    mean = jnp.mean(grad, axis=-1, keepdims=True)
    along = jnp.mean(grad * normal, axis=-1, keepdims=True)
    return scale * (grad - mean - normal * along)


def add_sums(sums, *values):
    @pl.when(pl.program_id(0) == 0)
    def _():
        sums[...] = jnp.zeros_like(sums)

    for at, value in enumerate(values):
        sums[at : at + 1, :] += jnp.sum(value, axis=0, keepdims=True)


def second_norm_kernel(normed, fed, cotangent, lines, result, grad_ref, low_ref, sums):
    normal, scale = norm_parts(normed[...] + fed[...] + lines[2:3, :])
    result[...] = (normal * lines[0:1, :] + lines[1:2, :]).astype(low)
    cotangent = cotangent[...].astype(f32)
    grad = norm_pull(normal, scale, lines[0:1, :], cotangent)
    grad_ref[...] = grad
    low_ref[...] = grad.astype(low)
    add_sums(sums, cotangent * normal, cotangent, grad)


def first_norm_kernel(summed, fed, total_grad, lines, grad_ref, low_ref, sums):
    normal, scale = norm_parts(summed[...])
    cotangent = fed[...] + total_grad[...]
    grad = norm_pull(normal, scale, lines[0:1, :], cotangent)
    grad_ref[...] = grad
    low_ref[...] = grad.astype(low)
    add_sums(sums, cotangent * normal, cotangent, grad)


def norm_call(kernel, arrays, lines, kinds, name):
    rows, dim = arrays[0].shape
    block = 256 if rows % 256 == 0 else 128
    part = pl.BlockSpec((block, dim), lambda i: (i, 0))
    return pl.pallas_call(
        kernel,
        grid=(rows // block,),
        in_specs=[part] * len(arrays) + [pl.BlockSpec(lines.shape, lambda i: (0, 0))],
        out_specs=[part] * len(kinds) + [pl.BlockSpec((3, dim), lambda i: (0, 0))],
        out_shape=[
            *[jax.ShapeDtypeStruct((rows, dim), kind) for kind in kinds],
            jax.ShapeDtypeStruct((3, dim), f32),
        ],
        compiler_params=kernel_params(),
        cost_estimate=pl.CostEstimate(
            flops=32 * rows * dim, bytes_accessed=36 * rows * dim, transcendentals=0
        ),
        name=name,
    )(*arrays, lines)


def feed_back_kernel(
    rows, ch, blocks, core, x, normed, up, down, slope, hidden,
    sum_ref, out_ref, sent_ref, own_ref, x_t, normed_t, pre_all,
):
    half = x_t.shape[0] // 2
    size = 2 * half // blocks

    @pl.when(pl.program_id(0) == 0)
    def _():
        out_ref[...] = jnp.zeros_like(out_ref)
        for source, turned in ((x, x_t), (normed, normed_t)):
            for first in range(0, blocks, 2):
                pair = source[:, first * size : (first + 2) * size].T
                for odd in range(2):
                    own = jnp.where(core[0] == odd, half, 0)
                    at = pl.multiple_of(own + first // 2 * size, size)
                    turned[pl.ds(at, size), :] = pair[odd * size : (odd + 1) * size]

    block = slope.shape[1]
    sums = jnp.zeros((8, block), f32)

    def finish(span, hidden_grad, sums):
        pre = hidden_grad * slope[span, :].astype(f32)
        sums = sums + jnp.sum(pre.reshape(ch // 8, 8, block), axis=0)
        pre = pre.astype(low)
        pre_all[span, :] = pre
        out_ref[span, :] += dot_nt(pre, up[...])
        return sums

    before = None
    for first in range(0, rows, ch):
        span = slice(first, first + ch)
        hidden_grad = dot(x[span, :], down[...])
        if before is not None:
            sums = finish(*before, sums)
        before = (span, hidden_grad)
    owners = (blocks // 2, size, block)
    sent_ref[:, 1] = dot(x_t[:half, :], hidden[...]).astype(low).reshape(owners)
    sums = finish(*before, sums)
    sum_ref[...] = jnp.sum(sums, axis=0, keepdims=True)
    own_ref[:, 1] = dot(x_t[half:, :], hidden[...]).reshape(owners)
    sent_ref[:, 0] = dot(normed_t[:half, :], pre_all[...]).astype(low).reshape(owners)
    own_ref[:, 0] = dot(normed_t[half:, :], pre_all[...]).reshape(owners)


def feed_back(core, blocks, x, normed, weights, slope, hidden, units, block=512, ch=512):
    rows, dim = x.shape
    groups = weights.shape[0]
    block = min(block, units)
    per = units // block
    ch = ch if rows % ch == 0 else rows
    every = groups * units
    weight = lambda skip: pl.BlockSpec(
        (None, dim, block), lambda i: (i // per, 0, skip * per + i % per)
    )
    part = pl.BlockSpec((rows, block), lambda i: (0, i))
    owners = (blocks // 2, 2, dim // blocks)
    half = pl.BlockSpec((None, *owners, block), lambda i: (i // per, 0, 0, 0, i % per))
    once = pl.BlockSpec((rows, dim), lambda i: (0, 0), pipeline_mode=pl.Buffered(1))
    return pl.pallas_call(
        functools.partial(feed_back_kernel, rows, ch, blocks),
        grid=(groups * per,),
        in_specs=[
            pl.BlockSpec(memory_space=pltpu.SMEM), once, once, weight(0), weight(1), part, part
        ],
        out_specs=[
            pl.BlockSpec((1, block), lambda i: (0, i)),
            pl.BlockSpec((rows, dim), lambda i: (0, 0)),
            half,
            half,
        ],
        out_shape=[
            jax.ShapeDtypeStruct((1, every), f32),
            jax.ShapeDtypeStruct((rows, dim), f32),
            jax.ShapeDtypeStruct((groups, *owners, units), low),
            jax.ShapeDtypeStruct((groups, *owners, units), f32),
        ],
        scratch_shapes=[
            pltpu.VMEM((dim, rows), low),
            pltpu.VMEM((dim, rows), low),
            pltpu.VMEM((rows, block), low),
        ],
        compiler_params=kernel_params(),
        cost_estimate=brief(8 * rows * dim * every),
        name="feed_back",
    )(core, x, normed, weights, weights, slope, hidden)


def bits_of(size):
    return size.bit_length() - 1


def swap(value, axis_name, mask):
    size = lax.axis_size(axis_name)
    return lax.ppermute(value, axis_name, [(i, i ^ mask) for i in range(size)])


def pick(value, index, axis):
    return lax.dynamic_index_in_dim(value, index, axis, keepdims=False)


def after(value, *others):
    return lax.optimization_barrier((value,) + others)[0]


def halve_parts(value, axis_name, bit, axis):
    mine = (lax.axis_index(axis_name) >> bit) & 1
    return pick(value, 1 - mine, axis).astype(jnp.bfloat16), pick(value, mine, axis)


def halve(value, axis_name, bit, axis):
    sent, kept = halve_parts(value, axis_name, bit, axis)
    return kept + swap(sent, axis_name, 1 << bit).astype(jnp.float32)


def chip_steps():
    return bits_of(lax.axis_size("dp")) - 1


def by_bits(value):
    return value.reshape((2,) * chip_steps() + (-1, value.shape[-1]))


def core_halves(rows_t):
    core = lax.axis_index("dp") & 1
    tokens = rows_t.shape[1]
    split = rows_t.reshape(lax.axis_size("dp") // 2, 2, -1, tokens)
    return pick(split, 1 - core, 1).reshape(-1, tokens), pick(split, core, 1).reshape(-1, tokens)


def core_first(halves, right):
    other, own = halves
    sent = jnp.dot(other, right, preferred_element_type=jnp.float32).astype(jnp.bfloat16)
    got = swap(sent, "dp", 1)
    return jnp.dot(own, right, preferred_element_type=jnp.float32) + got.astype(jnp.float32)


def over_chips(value):
    size = lax.axis_size("mp") * lax.axis_size("dp")
    groups = [[i for i in range(size) if i % 2 == core] for core in range(2)]
    return lax.psum_scatter(
        value, ("mp", "dp"), scatter_dimension=0, axis_index_groups=groups, tiled=True
    )


def over_mp_relative(blocks):
    blocks = list(blocks)
    for step in reversed(range(bits_of(len(blocks)))):
        size = 1 << step
        blocks = [
            blocks[j] + swap(blocks[j + size].astype(jnp.bfloat16), "mp", size).astype(jnp.float32)
            for j in range(size)
        ]
    return blocks[0]


def sum_steps():
    return [
        (name, 1 << step) for name in ("mp", "dp") for step in range(bits_of(lax.axis_size(name)))
    ]


def body(
    layer_input,
    out_cotangent,
    segment_ids,
    qkv_weight,
    out_weight,
    up_weight,
    down_weight,
    norm_gains,
    bias_rows,
    up_bias,
    qkv_moments,
    out_moments,
    up_moments,
    down_moments,
    gain_moments,
    bias_moments,
    up_bias_moments,
):
    mp = lax.axis_size("mp")
    me = lax.axis_index("mp")
    dp = lax.axis_size("dp")
    dp_me = lax.axis_index("dp")
    width = qkv_weight.shape[2]
    units = up_weight.shape[1]
    tokens, dim = layer_input.shape
    rows = tokens // mp
    pairs = width // PAIR
    heads_local = width // HEAD_DIM
    low = jnp.bfloat16
    block = min(512, tokens)
    column_start = me * width

    def relative(value, axis):
        shape = value.shape
        value = value.reshape(shape[:axis] + (mp, rows) + shape[axis + 1 :])
        parts = [pick(value, me ^ j, axis) for j in range(mp)]
        return jnp.concatenate(parts, axis=axis)

    qkv_low = qkv_weight.astype(low)
    by_pair = qkv_low.reshape(3, -1, pairs, PAIR).transpose(1, 2, 0, 3).reshape(-1, 3 * width)
    qkv_full = lax.all_gather(by_pair, "dp", axis=0, tiled=True)
    weight_set = jnp.concatenate(
        [up_weight.astype(low), down_weight.astype(low), out_weight.astype(low)], axis=1
    )
    inputs = relative(layer_input, 0)
    input_halves = core_halves(inputs.T)
    ids = relative(segment_ids.reshape(-1), 0)
    document = jnp.arange(PAIR, dtype=jnp.int32)
    same = ids[:, None] == document[None, :]
    key_marks = jnp.where(same | (document[None, :] > 2), 0.0, very_low).astype(low)
    query_marks = same.T.astype(low)
    head_bias = lax.dynamic_slice_in_dim(bias_rows[:2], column_start, width, 1)

    queries, queries_t, key_rows, keys_t, values_all, values_t = project(
        inputs, qkv_full, head_bias, key_marks
    )
    weight_set = after(weight_set, qkv_full, key_marks, query_marks, *input_halves)
    weights_all = lax.all_gather(weight_set, ("mp", "dp"), axis=0, tiled=True)
    weights_all = weights_all.reshape(mp, dim, -1)
    own_core = (dp_me & 1).astype(jnp.int32).reshape(1)

    calls = [(0, pairs - 1), (pairs - 1, 1)] if pairs > 1 else [(0, 1)]
    place = [(call, at) for call, (_, count) in enumerate(calls) for at in range(count)]
    saved, attended_rel, tops = [], [[] for _ in range(mp)], []
    for first, count in calls:
        probs, attended_t, attended, totals, maxima = attention_forward(
            key_rows, queries_t, query_marks, values_t, first, count, block
        )
        if first > 0:
            came = [parts[0] for parts in attended_rel[1:]]
            attended, maxima = lax.optimization_barrier((attended, maxima, *came))[:2]
        saved.append((probs, attended_t, totals))
        query_marks = after(query_marks, attended)
        tops.append(maxima)
        for j in range(mp):
            piece = attended[j * rows : (j + 1) * rows]
            attended_rel[j].append(piece if j == 0 else swap(piece, "mp", j))
    qkv_all = lax.all_gather(
        after(qkv_full, weights_all, totals), "mp", axis=0, tiled=False
    )
    head_max = jnp.max(jnp.concatenate(tops).reshape(heads_local, PAIR), axis=1)
    head_max = head_max * HEAD_DIM ** (-0.5)
    attended_all = jnp.concatenate([piece for parts in attended_rel for piece in parts], axis=1)

    out_rel = [pick(weights_all[:, :, 2 * units :], me ^ j, 0) for j in range(mp)]
    branch = times_transposed(attended_all, jnp.concatenate(out_rel, axis=1))
    summed = inputs[:rows].astype(jnp.float32) + branch + bias_rows[2]
    normed = norm_rows(summed, norm_gains[0], bias_rows[4])
    normed_low = normed.astype(low)
    hidden_low, slope, ffn_out = feed_forward(
        normed_low, weights_all, up_bias[None], units
    )
    second_lines = jnp.stack([norm_gains[1], bias_rows[5], bias_rows[3]])
    result, total_grad, total_low, second_sums = norm_call(
        second_norm_kernel,
        [normed, ffn_out, out_cotangent],
        second_lines,
        [low, jnp.float32, low],
        "second_norm",
    )
    total_low = after(total_low, qkv_all)
    up_bias_grad, feed_grad, sent, own = feed_back(
        own_core, dp, total_low, normed_low, weights_all, slope, hidden_low, units
    )
    feed_low = (own + swap(sent, "dp", 1).astype(jnp.float32)).astype(low)
    summed_grad, summed_low, first_sums = norm_call(
        first_norm_kernel,
        [summed, feed_grad, total_grad],
        norm_gains[:1],
        [jnp.float32, low],
        "first_norm",
    )
    grad_rel = [[None] * mp for _ in range(pairs)]
    for j in reversed(range(mp)):
        piece = jnp.dot(summed_low, out_rel[j], preferred_element_type=jnp.float32).astype(low)
        for pair in range(pairs):
            part = piece[:, pair * PAIR : (pair + 1) * PAIR]
            if j and pair:
                part = after(part, grad_rel[0][j])
            grad_rel[pair][j] = part if j == 0 else swap(part, "mp", j)
        summed_late = after(summed_low, piece) if j == mp - 1 else summed_late
    feed_part = over_chips(feed_low.reshape(-1, units))
    out_part = core_first(core_halves(summed_late.T), attended_all)

    slot = lax.broadcasted_iota(jnp.int32, (dp * mp, heads_local), 0)
    slots = jnp.where(slot == dp_me * mp + me, head_max[None], 0.0)
    slots = jnp.pad(slots.reshape(-1), (0, -slots.size % dim)).reshape(-1, dim)
    early = jnp.concatenate([first_sums, second_sums, up_bias_grad.reshape(-1, dim), slots])
    waiting = sum_steps()

    def add_step(value, *others):
        name, mask = waiting.pop(0)
        value = after(value, *others)
        return value + swap(value, name, mask)

    early = add_step(early)
    halves_other, halves_own = input_halves
    own_rows, got_rows = [], [[] for _ in range(mp - 1)]
    sent_pieces, qkv_pieces, bias_pieces = [], [], []
    chains, chained = [], 0

    def own_piece(pair, *others):
        grads, got = sent_pieces[pair]
        own_part = jnp.dot(after(halves_own, *others), grads, preferred_element_type=jnp.float32)
        return own_part + got.astype(jnp.float32)

    grads_low = None
    for pair, (call, at) in enumerate(place):
        probs, attended_t, totals = saved[call]
        ready = [feed_low, out_part, early] if pair == 0 else [early, grads_low, *sending]
        if pair > 1:
            ready += [rows_of[pair - 2] for rows_of in got_rows] + [qkv_pieces[pair - 2]]
        if len(qkv_pieces) > chained:
            fresh = qkv_pieces[chained:]
            fresh = [out_part, *fresh] if chained == 0 else fresh
            chains.append((0, by_bits(jnp.concatenate(fresh, axis=1))))
            chained = len(qkv_pieces)
        moving = []
        for step, value in chains:
            if step == chip_steps():
                moving.append((step, value, None))
                continue
            sent, kept = halve_parts(value, "dp", step + 1, chip_steps() - 1 - step)
            sent = after(sent, grads_low)
            ready.append(sent)
            moving.append((step + 1, kept, swap(sent, "dp", 2 << step)))
        grad_parts = list(grad_rel[pair])
        if pair > 0:
            grad_parts[0] = after(grad_parts[0], grads_low)
        grad_now = after(jnp.concatenate(grad_parts, axis=0), *ready)
        if waiting:
            early = add_step(early, *([] if grads_low is None else [grads_low]))
        grads_low, head_sums = attention_backward(
            probs, grad_now, attended_t, totals, queries, values_all, keys_t, pair, at
        )
        if pair == pairs - 1 and pair > 0:
            kept = [rows_of[pair - 1] for rows_of in got_rows]
            grads_low, head_sums = lax.optimization_barrier((grads_low, head_sums, *kept))[:2]
        bias_pieces.append(head_sums)
        if pair > 0:
            qkv_pieces.append(own_piece(pair - 1, grads_low))
        chains = [
            (step, kept if got is None else after(kept, grads_low) + got.astype(jnp.float32))
            for step, kept, got in moving
        ]
        own_rows.append(grads_low[:rows])
        sending = [grads_low[j * rows : (j + 1) * rows] for j in range(1, mp)]
        for j in range(1, mp):
            got_rows[j - 1].append(swap(sending[j - 1], "mp", j))
        sent = jnp.dot(halves_other, grads_low, preferred_element_type=jnp.float32).astype(low)
        sent_pieces.append((grads_low, swap(sent, "dp", 1)))
        sending.append(sent)
    qkv_pieces.append(own_piece(pairs - 1))
    while waiting:
        early = add_step(early)
    feed_rows = feed_part.shape[0] // 2
    up_sum = feed_part[:feed_rows].astype(jnp.float32)
    down_sum = feed_part[feed_rows:].astype(jnp.float32)

    input_grad = summed_grad + times_transposed(
        jnp.concatenate(own_rows, axis=1), qkv_full
    )
    last_parts = []
    for j in range(1, mp):
        others = pick(qkv_all, me ^ j, 0)
        parts = got_rows[j - 1]
        if pairs > 1:
            input_grad = input_grad + times_transposed(
                jnp.concatenate(parts[:-1], axis=1), others[:, : -3 * PAIR]
            )
        last_parts.append((parts[-1], others[:, -3 * PAIR :]))
    most_grad = input_grad
    for got, others in last_parts:
        input_grad = input_grad + times_transposed(got, others)
    early = after(early, most_grad)
    gain_sum = jnp.stack([early[0], early[3]])
    late_biases = jnp.stack([early[2], early[5], early[1], early[4]])
    unit_sum = early[6 : 6 + units * mp // dim].reshape(-1)
    group_max = early[6 + units * mp // dim :].reshape(-1)[: dp * mp * heads_local]
    group_max = jnp.max(group_max.reshape(dp, mp, heads_local), axis=0)
    local_max = pick(group_max, me, 0)
    fresh = qkv_pieces[chained:]
    fresh = [out_part, *fresh] if chained == 0 else fresh
    summing = by_bits(jnp.concatenate(fresh, axis=1))
    for step in range(chip_steps()):
        while chains and chains[-1][0] == step:
            summing = jnp.concatenate([chains.pop()[1], summing], axis=-1)
        summing = halve(summing, "dp", step + 1, chip_steps() - 1 - step)
        if step == 0:
            summing = after(summing, most_grad)
    summing = jnp.concatenate([value for _, value in chains] + [summing], axis=-1)
    out_sum = summing[:, : mp * width]
    qkv_sum = summing[:, mp * width :].reshape(-1, pairs, 3, PAIR)
    out_sum = over_mp_relative([out_sum[:, j * width : (j + 1) * width] for j in range(mp)])
    qkv_sum = qkv_sum.transpose(2, 0, 1, 3).reshape(3, -1, width)

    head_biases = lax.dynamic_update_slice_in_dim(
        jnp.zeros((2, width * mp), jnp.float32),
        jnp.concatenate(bias_pieces, axis=1),
        column_start,
        1,
    )
    for name, mask in sum_steps():
        head_biases = head_biases + swap(head_biases, name, mask)
    bias_sum = jnp.concatenate([head_biases, late_biases], axis=0)

    grad_scale = lax.rsqrt(jnp.float32(tokens * dp))
    step_value = jnp.float32(ADAM_STEP)
    new_qkv, next_qkv = adam_update(qkv_weight, qkv_moments, qkv_sum * grad_scale, step_value)
    new_out, next_out = adam_update(out_weight, out_moments, out_sum * grad_scale, step_value)
    new_up, next_up = adam_update(up_weight, up_moments, up_sum * grad_scale, step_value)
    new_down, next_down = adam_update(down_weight, down_moments, down_sum * grad_scale, step_value)
    new_gains, next_gains = adam_update(norm_gains, gain_moments, gain_sum * grad_scale, step_value)
    new_biases, next_biases = adam_update(
        bias_rows, bias_moments, bias_sum * grad_scale, step_value
    )
    new_up_bias, next_up_bias = adam_update(
        up_bias, up_bias_moments, unit_sum * grad_scale, step_value
    )
    factor = jnp.sqrt(clip_tau / jnp.maximum(local_max, clip_tau))
    column = jnp.repeat(factor, HEAD_DIM)
    scales = jnp.stack([column, column, jnp.ones_like(column)])[:, None, :]
    new_qkv = new_qkv * scales
    return (
        result.astype(jnp.bfloat16),
        input_grad,
        new_qkv,
        new_out,
        new_up,
        new_down,
        new_gains,
        new_biases,
        new_up_bias,
        next_qkv,
        next_out,
        next_up,
        next_down,
        next_gains,
        next_biases,
        next_up_bias,
    )


def solution(mesh):
    placed = (
        P("dp", None),
        P(("dp", "mp"), None),
        P("dp", None),
        P(None, "dp", "mp"),
        P("dp", "mp"),
        P("dp", "mp"),
        P("dp", "mp"),
        P(),
        P(),
        P(),
        P(None, None, "dp", "mp"),
        P(None, "dp", "mp"),
        P(None, "dp", "mp"),
        P(None, "dp", "mp"),
        P(),
        P(),
        P(),
    )
    return jax.shard_map(
        body,
        mesh=mesh,
        in_specs=placed,
        out_specs=(
            P(("dp", "mp"), None),
            P(("dp", "mp"), None),
            P(None, "dp", "mp"),
            P("dp", "mp"),
            P("dp", "mp"),
            P("dp", "mp"),
            P(),
            P(),
            P(),
            P(None, None, "dp", "mp"),
            P(None, "dp", "mp"),
            P(None, "dp", "mp"),
            P(None, "dp", "mp"),
            P(),
            P(),
            P(),
        ),
        check_vma=False,
    )
```

```python
import functools

import jax
import jax.numpy as jnp
from jax import lax
from jax.experimental import pallas as pl
from jax.experimental.pallas import tpu as pltpu
from jax.sharding import PartitionSpec as P

HEAD_DIM = 64
ADAM_STEP = 5
PAIR = 2 * HEAD_DIM
LOG2E = 1.4426950408889634

low = jnp.bfloat16
f32 = jnp.float32
very_low = -1e30
clip_tau = 5.0
learn_rate = 0.25
weight_decay = 0.1
moment_beta = 0.5
adam_epsilon = 1e-08


def norm_rows(values, gain_row, shift_row):
    center = values - jnp.mean(values, axis=-1, keepdims=True)
    spread = jnp.mean(center * center, axis=-1, keepdims=True)
    return center * lax.rsqrt(spread + 1e-05) * gain_row + shift_row


def times_transposed(left_side, right_side):
    return lax.dot_general(
        left_side, right_side, (((1,), (1,)), ((), ())), preferred_element_type=jnp.float32
    )


def adam_update(param, moments, grad, step_value):
    first_moment = moment_beta * moments[0] + (1.0 - moment_beta) * grad
    second_moment = moment_beta * moments[1] + (1.0 - moment_beta) * grad * grad
    correct = 1.0 - jnp.power(moment_beta, step_value)
    update = first_moment / correct / (jnp.sqrt(second_moment / correct) + adam_epsilon)
    return (
        param - learn_rate * (update + weight_decay * param),
        jnp.stack([first_moment, second_moment]),
    )


def dot(left, right):
    return lax.dot_general(left, right, (((1,), (0,)), ((), ())), preferred_element_type=f32)


def dot_nt(left, right):
    return lax.dot_general(left, right, (((1,), (1,)), ((), ())), preferred_element_type=f32)


def kernel_params(axes=1):
    return pltpu.CompilerParams(
        vmem_limit_bytes=58 * 2**20, dimension_semantics=("arbitrary",) * axes
    )


def brief(flops):
    return pl.CostEstimate(flops=flops // 16, bytes_accessed=2**20, transcendentals=0)


def project_kernel(pairs, x, weights, biases, marks, q_ref, qt_ref, k_ref, kt_ref, v_ref, vt_ref):
    for pair in range(pairs):
        span = slice(pair * PAIR, (pair + 1) * PAIR)
        every = dot(x[...], weights[:, 3 * pair * PAIR : 3 * (pair + 1) * PAIR])
        q = every[:, :PAIR] + biases[0:1, span]
        k = every[:, PAIR : 2 * PAIR]
        v = every[:, 2 * PAIR :] + biases[1:2, span]
        q_ref[:, span] = q.astype(low)
        qt_ref[span, :] = q.T.astype(low)
        k_ref[pair, :, :PAIR] = k.astype(low)
        k_ref[pair, :, PAIR:] = marks[...]
        kt_ref[span, :] = k.T.astype(low)
        v_ref[:, span] = v.astype(low)
        vt_ref[span, :] = v.T.astype(low)


def project(x, weights, biases, marks):
    tokens, dim = x.shape
    width = weights.shape[1] // 3
    pairs = width // PAIR
    block = min(512, tokens)
    rows = lambda n: pl.BlockSpec((block, n), lambda i: (i, 0))
    columns = pl.BlockSpec((width, block), lambda i: (0, i))
    natural = jax.ShapeDtypeStruct((tokens, width), low)
    turned = jax.ShapeDtypeStruct((width, tokens), low)
    return pl.pallas_call(
        functools.partial(project_kernel, pairs),
        grid=(tokens // block,),
        in_specs=[
            rows(dim),
            pl.BlockSpec((dim, 3 * width), lambda i: (0, 0)),
            pl.BlockSpec((2, width), lambda i: (0, 0)),
            rows(PAIR),
        ],
        out_specs=[
            rows(width),
            columns,
            pl.BlockSpec((pairs, block, 2 * PAIR), lambda i: (0, i, 0)),
            columns,
            rows(width),
            columns,
        ],
        out_shape=[
            natural,
            turned,
            jax.ShapeDtypeStruct((pairs, tokens, 2 * PAIR), low),
            turned,
            natural,
            turned,
        ],
        compiler_params=kernel_params(),
        cost_estimate=brief(6 * tokens * dim * width),
        name="project",
    )(x, weights, biases, marks)


def forward_kernel(
    bq, ch, tokens, k_cur, k_nxt, q_cur, q_nxt, s_cur, s_nxt, vt,
    p_ref, ot_ref, o_ref, l_ref, m_ref, score_a, score_b, max_a, max_b,
):
    zeros = jnp.zeros((HEAD_DIM, bq), low)
    factor = f32(LOG2E * HEAD_DIM**-0.5)
    steps = tokens // ch
    nq = tokens // bq

    def query_rows(q_ref, marks, head):
        q = q_ref[head * HEAD_DIM : (head + 1) * HEAD_DIM, :]
        parts = [q, zeros] if head == 0 else [zeros, q]
        return jnp.concatenate(parts + [marks[...]], axis=0)

    def scores(keys, q, out, step, top):
        part = dot(keys[step * ch : (step + 1) * ch, :], q)
        out[step * ch : (step + 1) * ch, :] = part
        return jnp.maximum(top, jnp.max(part.reshape(ch // 8, 8, bq), axis=0))

    def finish(top, out):
        out[...] = jnp.broadcast_to(jnp.max(top, axis=0, keepdims=True), (8, bq))

    lowest = jnp.full((8, bq), -3e38, f32)

    @pl.when(pl.program_id(0) == 0)
    def _():
        q = query_rows(q_cur, s_cur, 0)
        top = lowest
        for step in range(steps):
            top = scores(k_cur, q, score_a, step, top)
        finish(top, max_a)

    def phase(head, s_in, m_in, keys, q, s_out, m_out):
        top_row = m_in[0:1, :]
        top = lowest
        sums = jnp.zeros((8, bq), f32)
        total = jnp.zeros((HEAD_DIM, bq), f32)
        for step in range(steps):
            span = slice(step * ch, (step + 1) * ch)
            top = scores(keys, q, s_out, step, top)
            p = jnp.exp2((s_in[span, :] - top_row) * factor)
            sums = sums + jnp.sum(p.reshape(ch // 8, 8, bq), axis=0)
            p_low = p.astype(low)
            p_ref[0, head, 0, span, :] = p_low
            total = total + dot(vt[head * HEAD_DIM : (head + 1) * HEAD_DIM, span], p_low)
        finish(top, m_out)
        row_sum = jnp.sum(sums, axis=0, keepdims=True)
        l_ref[0, head : head + 1, :] = row_sum
        best = top_row[:, :PAIR]
        for first in range(PAIR, bq, PAIR):
            best = jnp.maximum(best, top_row[:, first : first + PAIR])
        here = jnp.where(pl.program_id(0) % nq == 0, lowest[0:1, :PAIR], m_ref[0, head : head + 1, :])
        m_ref[0, head : head + 1, :] = jnp.maximum(here, best)
        return total / row_sum

    first = phase(0, score_a, max_a, k_cur, query_rows(q_cur, s_cur, 1), score_b, max_b)
    second = phase(1, score_b, max_b, k_nxt, query_rows(q_nxt, s_nxt, 0), score_a, max_a)
    both = jnp.concatenate([first, second], axis=0)
    ot_ref[...] = both
    o_ref[...] = both.T.astype(low)


def attention_forward(keys, q_t, marks_t, v_t, first, pairs, bq, ch=512):
    _, tokens, _ = keys.shape
    nq = tokens // bq
    ch = min(ch, tokens)
    count = pairs * nq
    now = lambda i: i
    later = lambda i: jnp.minimum(i + 1, count - 1)
    key_spec = lambda at: pl.BlockSpec(
        (None, tokens, 2 * PAIR), lambda i: (first + at(i) // nq, 0, 0)
    )
    query_spec = lambda at: pl.BlockSpec((PAIR, bq), lambda i: (first + at(i) // nq, at(i) % nq))
    mark_spec = lambda at: pl.BlockSpec((PAIR, bq), lambda i: (0, at(i) % nq))
    row_spec = pl.BlockSpec((1, 2, bq), lambda i: (i // nq, 0, i % nq))
    size = 2 * pairs * tokens * tokens
    return pl.pallas_call(
        functools.partial(forward_kernel, bq, ch, tokens),
        grid=(count,),
        in_specs=[
            key_spec(now), key_spec(later), query_spec(now), query_spec(later),
            mark_spec(now), mark_spec(later),
            pl.BlockSpec((PAIR, tokens), lambda i: (first + i // nq, 0)),
        ],
        out_specs=[
            pl.BlockSpec((1, 2, 1, tokens, bq), lambda i: (i // nq, 0, i % nq, 0, 0)),
            pl.BlockSpec((PAIR, bq), lambda i: (i // nq, i % nq)),
            pl.BlockSpec((bq, PAIR), lambda i: (i % nq, i // nq)),
            row_spec,
            pl.BlockSpec((1, 2, PAIR), lambda i: (i // nq, 0, 0)),
        ],
        out_shape=[
            jax.ShapeDtypeStruct((pairs, 2, nq, tokens, bq), low),
            jax.ShapeDtypeStruct((pairs * PAIR, tokens), f32),
            jax.ShapeDtypeStruct((tokens, pairs * PAIR), low),
            jax.ShapeDtypeStruct((pairs, 2, tokens), f32),
            jax.ShapeDtypeStruct((pairs, 2, PAIR), f32),
        ],
        scratch_shapes=[
            pltpu.VMEM((tokens, bq), f32),
            pltpu.VMEM((tokens, bq), f32),
            pltpu.VMEM((8, bq), f32),
            pltpu.VMEM((8, bq), f32),
        ],
        compiler_params=kernel_params(),
        cost_estimate=brief(16 * HEAD_DIM * size),
        name="attend",
    )(keys, keys, q_t, q_t, marks_t, marks_t, v_t)


def backward_kernel(
    bq, ch, tokens, p_ref, grad, out_t, totals, q, v, kt, g_ref, b_ref, key_acc, value_acc, sums
):
    step_q = pl.program_id(0)

    @pl.when(step_q == 0)
    def _():
        key_acc[...] = jnp.zeros_like(key_acc)
        value_acc[...] = jnp.zeros_like(value_acc)
        sums[...] = jnp.zeros_like(sums)

    zeros = jnp.zeros((HEAD_DIM, bq), low)
    scale = f32(HEAD_DIM**-0.5)
    lane = lax.broadcasted_iota(jnp.int32, (bq, PAIR), 1)

    def diagonal(x):
        zero = jnp.zeros_like(x)
        return jnp.concatenate(
            [jnp.where(lane < HEAD_DIM, x, zero), jnp.where(lane >= HEAD_DIM, x, zero)], axis=0
        )

    grad_t = grad[...].astype(f32).T
    scaled_t, deltas = [], []
    for head in range(2):
        inverse = 1.0 / totals[0, head : head + 1, :]
        span = slice(head * HEAD_DIM, (head + 1) * HEAD_DIM)
        part = grad_t[span] * inverse
        deltas.append(jnp.sum(part * out_t[span, :], axis=0, keepdims=True))
        scaled_t.append(part)
    scaled = jnp.concatenate(scaled_t, axis=0).T.astype(low)
    grad_rows = diagonal(scaled)
    query_rows = diagonal(q[...])
    grad_columns = [
        jnp.concatenate([scaled_t[0].astype(low), zeros], axis=0),
        jnp.concatenate([zeros, scaled_t[1].astype(low)], axis=0),
    ]
    query_grads = [jnp.zeros((HEAD_DIM, bq), f32) for _ in range(2)]
    for step in range(tokens // ch):
        span = slice(step * ch, (step + 1) * ch)
        values = v[span, :]
        probs, score_grads = [], []
        for head in range(2):
            prob_grad = dot(values, grad_columns[head])
            p = p_ref[0, head, 0, span, :]
            score_grad = (p.astype(f32) * (prob_grad - deltas[head])).astype(low)
            probs.append(p)
            score_grads.append(score_grad)
            query_grads[head] = query_grads[head] + dot(
                kt[head * HEAD_DIM : (head + 1) * HEAD_DIM, span], score_grad
            )
        value_acc[span, :] += dot(jnp.concatenate(probs, axis=1), grad_rows)
        key_acc[span, :] += dot(jnp.concatenate(score_grads, axis=1), query_rows)
    query_grad = jnp.concatenate(query_grads, axis=0).T * scale
    g_ref[pl.ds(pl.multiple_of(step_q * bq, bq), bq), 0:PAIR] = query_grad.astype(low)
    sums[...] += jnp.sum(query_grad.reshape(bq // 8, 8, PAIR), axis=0)

    @pl.when(step_q == pl.num_programs(0) - 1)
    def _():
        g_ref[:, PAIR : 2 * PAIR] = (key_acc[...] * scale).astype(low)
        value_grad = value_acc[...]
        g_ref[:, 2 * PAIR :] = value_grad.astype(low)
        b_ref[0:1, :] = jnp.sum(sums[...], axis=0, keepdims=True)
        b_ref[1:2, :] = jnp.sum(value_grad, axis=0, keepdims=True)


def attention_backward(probs, grad, out_t, totals, q, v, k_t, pair, at, ch=1536):
    _, _, nq, tokens, bq = probs.shape
    ch = min(ch, tokens)
    size = 2 * tokens * tokens
    return pl.pallas_call(
        functools.partial(backward_kernel, bq, ch, tokens),
        grid=(nq,),
        in_specs=[
            pl.BlockSpec((1, 2, 1, tokens, bq), lambda i: (at, 0, i, 0, 0)),
            pl.BlockSpec((bq, PAIR), lambda i: (i, 0)),
            pl.BlockSpec((PAIR, bq), lambda i: (at, i)),
            pl.BlockSpec((1, 2, bq), lambda i: (at, 0, i)),
            pl.BlockSpec((bq, PAIR), lambda i: (i, pair)),
            pl.BlockSpec((tokens, PAIR), lambda i: (0, pair)),
            pl.BlockSpec((PAIR, tokens), lambda i: (pair, 0)),
        ],
        out_specs=[
            pl.BlockSpec((tokens, 3 * PAIR), lambda i: (0, 0)),
            pl.BlockSpec((2, PAIR), lambda i: (0, 0)),
        ],
        out_shape=[
            jax.ShapeDtypeStruct((tokens, 3 * PAIR), low),
            jax.ShapeDtypeStruct((2, PAIR), f32),
        ],
        scratch_shapes=[
            pltpu.VMEM((tokens, PAIR), f32),
            pltpu.VMEM((tokens, PAIR), f32),
            pltpu.VMEM((8, PAIR), f32),
        ],
        compiler_params=kernel_params(),
        cost_estimate=brief(32 * HEAD_DIM * size),
        name="attend_back",
    )(probs, grad, out_t, totals, q, v, k_t)


def gelu_and_slope(x):
    size = jnp.abs(x) * f32(0.7071067811865476)
    t = 1.0 / (1.0 + f32(0.3275911) * size)
    bell = jnp.exp2(x * x * f32(-0.5 * LOG2E))
    poly = f32(1.061405429 / 2)
    for coefficient in (-1.453152027, 1.421413741, -0.284496736, 0.254829592):
        poly = poly * t + f32(coefficient / 2)
    tail = poly * t * bell
    phi = jnp.where(x >= 0, 1.0 - tail, tail)
    return x * phi, phi + x * bell * f32(0.3989422804014327)


def feed_kernel(rows, ch, x, up, down, bias, hidden_ref, slope_ref, out_ref):
    @pl.when(pl.program_id(0) == 0)
    def _():
        out_ref[...] = jnp.zeros_like(out_ref)

    def finish(span, pre):
        hidden, slope = gelu_and_slope(pre + bias[...])
        hidden = hidden.astype(low)
        hidden_ref[span, :] = hidden
        slope_ref[span, :] = slope.astype(low)
        out_ref[span, :] += dot_nt(hidden, down[...])

    before = None
    for first in range(0, rows, ch):
        span = slice(first, first + ch)
        pre = dot(x[span, :], up[...])
        if before is not None:
            finish(*before)
        before = (span, pre)
    finish(*before)


def feed_forward(x, weights, bias, units, block=1024, ch=512):
    rows, dim = x.shape
    groups = weights.shape[0]
    block = min(block, units)
    per = units // block
    ch = ch if rows % ch == 0 else rows
    every = groups * units
    weight = lambda skip: pl.BlockSpec(
        (None, dim, block), lambda i: (i // per, 0, skip * per + i % per)
    )
    part = pl.BlockSpec((rows, block), lambda i: (0, i))
    whole = pl.BlockSpec((rows, dim), lambda i: (0, 0))
    return pl.pallas_call(
        functools.partial(feed_kernel, rows, ch),
        grid=(groups * per,),
        in_specs=[whole, weight(0), weight(1), pl.BlockSpec((1, block), lambda i: (0, i))],
        out_specs=[part, part, whole],
        out_shape=[
            jax.ShapeDtypeStruct((rows, every), low),
            jax.ShapeDtypeStruct((rows, every), low),
            jax.ShapeDtypeStruct((rows, dim), f32),
        ],
        compiler_params=kernel_params(),
        cost_estimate=pl.CostEstimate(
            flops=4 * rows * dim * every, bytes_accessed=8 * dim * every, transcendentals=0
        ),
        name="feed",
    )(x, weights, weights, bias)


def norm_parts(values):
    center = values - jnp.mean(values, axis=-1, keepdims=True)
    scale = lax.rsqrt(jnp.mean(center * center, axis=-1, keepdims=True) + 1e-05)
    return center * scale, scale


def norm_pull(normal, scale, gain, cotangent):
    grad = cotangent * gain
    mean = jnp.mean(grad, axis=-1, keepdims=True)
    along = jnp.mean(grad * normal, axis=-1, keepdims=True)
    return scale * (grad - mean - normal * along)


def add_sums(sums, *values):
    @pl.when(pl.program_id(0) == 0)
    def _():
        sums[...] = jnp.zeros_like(sums)

    for at, value in enumerate(values):
        sums[at : at + 1, :] += jnp.sum(value, axis=0, keepdims=True)


def second_norm_kernel(normed, fed, cotangent, lines, result, grad_ref, low_ref, sums):
    normal, scale = norm_parts(normed[...] + fed[...] + lines[2:3, :])
    result[...] = (normal * lines[0:1, :] + lines[1:2, :]).astype(low)
    cotangent = cotangent[...].astype(f32)
    grad = norm_pull(normal, scale, lines[0:1, :], cotangent)
    grad_ref[...] = grad
    low_ref[...] = grad.astype(low)
    add_sums(sums, cotangent * normal, cotangent, grad)


def first_norm_kernel(summed, fed, total_grad, lines, grad_ref, low_ref, sums):
    normal, scale = norm_parts(summed[...])
    cotangent = fed[...] + total_grad[...]
    grad = norm_pull(normal, scale, lines[0:1, :], cotangent)
    grad_ref[...] = grad
    low_ref[...] = grad.astype(low)
    add_sums(sums, cotangent * normal, cotangent, grad)


def norm_call(kernel, arrays, lines, kinds, name):
    rows, dim = arrays[0].shape
    block = 256 if rows % 256 == 0 else 128
    part = pl.BlockSpec((block, dim), lambda i: (i, 0))
    return pl.pallas_call(
        kernel,
        grid=(rows // block,),
        in_specs=[part] * len(arrays) + [pl.BlockSpec(lines.shape, lambda i: (0, 0))],
        out_specs=[part] * len(kinds) + [pl.BlockSpec((3, dim), lambda i: (0, 0))],
        out_shape=[
            *[jax.ShapeDtypeStruct((rows, dim), kind) for kind in kinds],
            jax.ShapeDtypeStruct((3, dim), f32),
        ],
        compiler_params=kernel_params(),
        cost_estimate=pl.CostEstimate(
            flops=32 * rows * dim, bytes_accessed=36 * rows * dim, transcendentals=0
        ),
        name=name,
    )(*arrays, lines)


def feed_back_kernel(
    rows, ch, blocks, core, x, normed, up, down, slope, hidden,
    sum_ref, out_ref, sent_ref, own_ref, x_t, normed_t, pre_all,
):
    half = x_t.shape[0] // 2
    size = 2 * half // blocks

    @pl.when(pl.program_id(0) == 0)
    def _():
        out_ref[...] = jnp.zeros_like(out_ref)
        for source, turned in ((x, x_t), (normed, normed_t)):
            for first in range(0, blocks, 2):
                pair = source[:, first * size : (first + 2) * size].T
                for odd in range(2):
                    own = jnp.where(core[0] == odd, half, 0)
                    at = pl.multiple_of(own + first // 2 * size, size)
                    turned[pl.ds(at, size), :] = pair[odd * size : (odd + 1) * size]

    block = slope.shape[1]
    sums = jnp.zeros((8, block), f32)

    def finish(span, hidden_grad, sums):
        pre = hidden_grad * slope[span, :].astype(f32)
        sums = sums + jnp.sum(pre.reshape(ch // 8, 8, block), axis=0)
        pre = pre.astype(low)
        pre_all[span, :] = pre
        out_ref[span, :] += dot_nt(pre, up[...])
        return sums

    before = None
    for first in range(0, rows, ch):
        span = slice(first, first + ch)
        hidden_grad = dot(x[span, :], down[...])
        if before is not None:
            sums = finish(*before, sums)
        before = (span, hidden_grad)
    owners = (blocks // 2, size, block)
    sent_ref[:, 1] = dot(x_t[:half, :], hidden[...]).astype(low).reshape(owners)
    sums = finish(*before, sums)
    sum_ref[...] = jnp.sum(sums, axis=0, keepdims=True)
    own_ref[:, 1] = dot(x_t[half:, :], hidden[...]).reshape(owners)
    sent_ref[:, 0] = dot(normed_t[:half, :], pre_all[...]).astype(low).reshape(owners)
    own_ref[:, 0] = dot(normed_t[half:, :], pre_all[...]).reshape(owners)


def feed_back(core, blocks, x, normed, weights, slope, hidden, units, block=512, ch=512):
    rows, dim = x.shape
    groups = weights.shape[0]
    block = min(block, units)
    per = units // block
    ch = ch if rows % ch == 0 else rows
    every = groups * units
    weight = lambda skip: pl.BlockSpec(
        (None, dim, block), lambda i: (i // per, 0, skip * per + i % per)
    )
    part = pl.BlockSpec((rows, block), lambda i: (0, i))
    owners = (blocks // 2, 2, dim // blocks)
    half = pl.BlockSpec((None, *owners, block), lambda i: (i // per, 0, 0, 0, i % per))
    once = pl.BlockSpec((rows, dim), lambda i: (0, 0), pipeline_mode=pl.Buffered(1))
    return pl.pallas_call(
        functools.partial(feed_back_kernel, rows, ch, blocks),
        grid=(groups * per,),
        in_specs=[
            pl.BlockSpec(memory_space=pltpu.SMEM), once, once, weight(0), weight(1), part, part
        ],
        out_specs=[
            pl.BlockSpec((1, block), lambda i: (0, i)),
            pl.BlockSpec((rows, dim), lambda i: (0, 0)),
            half,
            half,
        ],
        out_shape=[
            jax.ShapeDtypeStruct((1, every), f32),
            jax.ShapeDtypeStruct((rows, dim), f32),
            jax.ShapeDtypeStruct((groups, *owners, units), low),
            jax.ShapeDtypeStruct((groups, *owners, units), f32),
        ],
        scratch_shapes=[
            pltpu.VMEM((dim, rows), low),
            pltpu.VMEM((dim, rows), low),
            pltpu.VMEM((rows, block), low),
        ],
        compiler_params=kernel_params(),
        cost_estimate=brief(8 * rows * dim * every),
        name="feed_back",
    )(core, x, normed, weights, weights, slope, hidden)


def bits_of(size):
    return size.bit_length() - 1


def swap(value, axis_name, mask):
    size = lax.axis_size(axis_name)
    return lax.ppermute(value, axis_name, [(i, i ^ mask) for i in range(size)])


def pick(value, index, axis):
    return lax.dynamic_index_in_dim(value, index, axis, keepdims=False)


def after(value, *others):
    return lax.optimization_barrier((value,) + others)[0]


def halve_parts(value, axis_name, bit, axis):
    mine = (lax.axis_index(axis_name) >> bit) & 1
    return pick(value, 1 - mine, axis).astype(jnp.bfloat16), pick(value, mine, axis)


def halve(value, axis_name, bit, axis):
    sent, kept = halve_parts(value, axis_name, bit, axis)
    return kept + swap(sent, axis_name, 1 << bit).astype(jnp.float32)


def chip_steps():
    return bits_of(lax.axis_size("dp")) - 1


def by_bits(value):
    return value.reshape((2,) * chip_steps() + (-1, value.shape[-1]))


def core_halves(rows_t):
    core = lax.axis_index("dp") & 1
    tokens = rows_t.shape[1]
    split = rows_t.reshape(lax.axis_size("dp") // 2, 2, -1, tokens)
    return pick(split, 1 - core, 1).reshape(-1, tokens), pick(split, core, 1).reshape(-1, tokens)


def core_first(halves, right):
    other, own = halves
    sent = jnp.dot(other, right, preferred_element_type=jnp.float32).astype(jnp.bfloat16)
    got = swap(sent, "dp", 1)
    return jnp.dot(own, right, preferred_element_type=jnp.float32) + got.astype(jnp.float32)


def over_chips(value):
    size = lax.axis_size("mp") * lax.axis_size("dp")
    groups = [[i for i in range(size) if i % 2 == core] for core in range(2)]
    return lax.psum_scatter(
        value, ("mp", "dp"), scatter_dimension=0, axis_index_groups=groups, tiled=True
    )


def over_mp_relative(blocks):
    blocks = list(blocks)
    for step in reversed(range(bits_of(len(blocks)))):
        size = 1 << step
        blocks = [
            blocks[j] + swap(blocks[j + size].astype(jnp.bfloat16), "mp", size).astype(jnp.float32)
            for j in range(size)
        ]
    return blocks[0]


def sum_steps():
    return [
        (name, 1 << step) for name in ("mp", "dp") for step in range(bits_of(lax.axis_size(name)))
    ]


def body(
    layer_input,
    out_cotangent,
    segment_ids,
    qkv_weight,
    out_weight,
    up_weight,
    down_weight,
    norm_gains,
    bias_rows,
    up_bias,
    qkv_moments,
    out_moments,
    up_moments,
    down_moments,
    gain_moments,
    bias_moments,
    up_bias_moments,
):
    mp = lax.axis_size("mp")
    me = lax.axis_index("mp")
    dp = lax.axis_size("dp")
    dp_me = lax.axis_index("dp")
    width = qkv_weight.shape[2]
    units = up_weight.shape[1]
    tokens, dim = layer_input.shape
    rows = tokens // mp
    pairs = width // PAIR
    heads_local = width // HEAD_DIM
    low = jnp.bfloat16
    block = min(512, tokens)
    column_start = me * width

    def relative(value, axis):
        shape = value.shape
        value = value.reshape(shape[:axis] + (mp, rows) + shape[axis + 1 :])
        parts = [pick(value, me ^ j, axis) for j in range(mp)]
        return jnp.concatenate(parts, axis=axis)

    qkv_low = qkv_weight.astype(low)
    by_pair = qkv_low.reshape(3, -1, pairs, PAIR).transpose(1, 2, 0, 3).reshape(-1, 3 * width)
    qkv_full = lax.all_gather(by_pair, "dp", axis=0, tiled=True)
    weight_set = jnp.concatenate(
        [up_weight.astype(low), down_weight.astype(low), out_weight.astype(low)], axis=1
    )
    inputs = relative(layer_input, 0)
    input_halves = core_halves(inputs.T)
    ids = relative(segment_ids.reshape(-1), 0)
    document = jnp.arange(PAIR, dtype=jnp.int32)
    same = ids[:, None] == document[None, :]
    key_marks = jnp.where(same | (document[None, :] > 2), 0.0, very_low).astype(low)
    query_marks = same.T.astype(low)
    head_bias = lax.dynamic_slice_in_dim(bias_rows[:2], column_start, width, 1)

    queries, queries_t, key_rows, keys_t, values_all, values_t = project(
        inputs, qkv_full, head_bias, key_marks
    )
    weight_set = after(weight_set, qkv_full, key_marks, query_marks, *input_halves)
    weights_all = lax.all_gather(weight_set, ("mp", "dp"), axis=0, tiled=True)
    weights_all = weights_all.reshape(mp, dim, -1)
    own_core = (dp_me & 1).astype(jnp.int32).reshape(1)

    calls = [(0, pairs - 1), (pairs - 1, 1)] if pairs > 1 else [(0, 1)]
    place = [(call, at) for call, (_, count) in enumerate(calls) for at in range(count)]
    saved, attended_rel, tops = [], [[] for _ in range(mp)], []
    for first, count in calls:
        probs, attended_t, attended, totals, maxima = attention_forward(
            key_rows, queries_t, query_marks, values_t, first, count, block
        )
        if first > 0:
            came = [parts[0] for parts in attended_rel[1:]]
            attended, maxima = lax.optimization_barrier((attended, maxima, *came))[:2]
        saved.append((probs, attended_t, totals))
        query_marks = after(query_marks, attended)
        tops.append(maxima)
        for j in range(mp):
            piece = attended[j * rows : (j + 1) * rows]
            attended_rel[j].append(piece if j == 0 else swap(piece, "mp", j))
    qkv_all = lax.all_gather(
        after(qkv_full, weights_all, totals), "mp", axis=0, tiled=False
    )
    head_max = jnp.max(jnp.concatenate(tops).reshape(heads_local, PAIR), axis=1)
    head_max = head_max * HEAD_DIM ** (-0.5)
    attended_all = jnp.concatenate([piece for parts in attended_rel for piece in parts], axis=1)

    out_rel = [pick(weights_all[:, :, 2 * units :], me ^ j, 0) for j in range(mp)]
    branch = times_transposed(attended_all, jnp.concatenate(out_rel, axis=1))
    summed = inputs[:rows].astype(jnp.float32) + branch + bias_rows[2]
    normed = norm_rows(summed, norm_gains[0], bias_rows[4])
    normed_low = normed.astype(low)
    hidden_low, slope, ffn_out = feed_forward(
        normed_low, weights_all, up_bias[None], units
    )
    second_lines = jnp.stack([norm_gains[1], bias_rows[5], bias_rows[3]])
    result, total_grad, total_low, second_sums = norm_call(
        second_norm_kernel,
        [normed, ffn_out, out_cotangent],
        second_lines,
        [low, jnp.float32, low],
        "second_norm",
    )
    total_low = after(total_low, qkv_all)
    up_bias_grad, feed_grad, sent, own = feed_back(
        own_core, dp, total_low, normed_low, weights_all, slope, hidden_low, units
    )
    feed_low = (own + swap(sent, "dp", 1).astype(jnp.float32)).astype(low)
    summed_grad, summed_low, first_sums = norm_call(
        first_norm_kernel,
        [summed, feed_grad, total_grad],
        norm_gains[:1],
        [jnp.float32, low],
        "first_norm",
    )
    grad_rel = [[None] * mp for _ in range(pairs)]
    for j in reversed(range(mp)):
        piece = jnp.dot(summed_low, out_rel[j], preferred_element_type=jnp.float32).astype(low)
        for pair in range(pairs):
            part = piece[:, pair * PAIR : (pair + 1) * PAIR]
            if j and pair:
                part = after(part, grad_rel[0][j])
            grad_rel[pair][j] = part if j == 0 else swap(part, "mp", j)
        summed_late = after(summed_low, piece) if j == mp - 1 else summed_late
    feed_part = over_chips(feed_low.reshape(-1, units))
    out_part = core_first(core_halves(summed_late.T), attended_all)

    slot = lax.broadcasted_iota(jnp.int32, (dp * mp, heads_local), 0)
    slots = jnp.where(slot == dp_me * mp + me, head_max[None], 0.0)
    slots = jnp.pad(slots.reshape(-1), (0, -slots.size % dim)).reshape(-1, dim)
    early = jnp.concatenate([first_sums, second_sums, up_bias_grad.reshape(-1, dim), slots])
    waiting = sum_steps()

    def add_step(value, *others):
        name, mask = waiting.pop(0)
        value = after(value, *others)
        return value + swap(value, name, mask)

    early = add_step(early)
    halves_other, halves_own = input_halves
    own_rows, got_rows = [], [[] for _ in range(mp - 1)]
    sent_pieces, qkv_pieces, bias_pieces = [], [], []
    chains, chained = [], 0

    def own_piece(pair, *others):
        grads, got = sent_pieces[pair]
        own_part = jnp.dot(after(halves_own, *others), grads, preferred_element_type=jnp.float32)
        return own_part + got.astype(jnp.float32)

    grads_low = None
    for pair, (call, at) in enumerate(place):
        probs, attended_t, totals = saved[call]
        ready = [feed_low, out_part, early] if pair == 0 else [early, grads_low, *sending]
        if pair > 1:
            ready += [rows_of[pair - 2] for rows_of in got_rows] + [qkv_pieces[pair - 2]]
        if len(qkv_pieces) > chained:
            fresh = qkv_pieces[chained:]
            fresh = [out_part, *fresh] if chained == 0 else fresh
            chains.append((0, by_bits(jnp.concatenate(fresh, axis=1))))
            chained = len(qkv_pieces)
        moving = []
        for step, value in chains:
            if step == chip_steps():
                moving.append((step, value, None))
                continue
            sent, kept = halve_parts(value, "dp", step + 1, chip_steps() - 1 - step)
            sent = after(sent, grads_low)
            ready.append(sent)
            moving.append((step + 1, kept, swap(sent, "dp", 2 << step)))
        grad_parts = list(grad_rel[pair])
        if pair > 0:
            grad_parts[0] = after(grad_parts[0], grads_low)
        grad_now = after(jnp.concatenate(grad_parts, axis=0), *ready)
        if waiting:
            early = add_step(early, *([] if grads_low is None else [grads_low]))
        grads_low, head_sums = attention_backward(
            probs, grad_now, attended_t, totals, queries, values_all, keys_t, pair, at
        )
        if pair == pairs - 1 and pair > 0:
            kept = [rows_of[pair - 1] for rows_of in got_rows]
            grads_low, head_sums = lax.optimization_barrier((grads_low, head_sums, *kept))[:2]
        bias_pieces.append(head_sums)
        if pair > 0:
            qkv_pieces.append(own_piece(pair - 1, grads_low))
        chains = [
            (step, kept if got is None else after(kept, grads_low) + got.astype(jnp.float32))
            for step, kept, got in moving
        ]
        own_rows.append(grads_low[:rows])
        sending = [grads_low[j * rows : (j + 1) * rows] for j in range(1, mp)]
        for j in range(1, mp):
            got_rows[j - 1].append(swap(sending[j - 1], "mp", j))
        sent = jnp.dot(halves_other, grads_low, preferred_element_type=jnp.float32).astype(low)
        sent_pieces.append((grads_low, swap(sent, "dp", 1)))
        sending.append(sent)
    qkv_pieces.append(own_piece(pairs - 1))
    while waiting:
        early = add_step(early)
    feed_rows = feed_part.shape[0] // 2
    up_sum = feed_part[:feed_rows].astype(jnp.float32)
    down_sum = feed_part[feed_rows:].astype(jnp.float32)

    input_grad = summed_grad + times_transposed(
        jnp.concatenate(own_rows, axis=1), qkv_full
    )
    last_parts = []
    for j in range(1, mp):
        others = pick(qkv_all, me ^ j, 0)
        parts = got_rows[j - 1]
        if pairs > 1:
            input_grad = input_grad + times_transposed(
                jnp.concatenate(parts[:-1], axis=1), others[:, : -3 * PAIR]
            )
        last_parts.append((parts[-1], others[:, -3 * PAIR :]))
    most_grad = input_grad
    for got, others in last_parts:
        input_grad = input_grad + times_transposed(got, others)
    early = after(early, most_grad)
    gain_sum = jnp.stack([early[0], early[3]])
    late_biases = jnp.stack([early[2], early[5], early[1], early[4]])
    unit_sum = early[6 : 6 + units * mp // dim].reshape(-1)
    group_max = early[6 + units * mp // dim :].reshape(-1)[: dp * mp * heads_local]
    group_max = jnp.max(group_max.reshape(dp, mp, heads_local), axis=0)
    local_max = pick(group_max, me, 0)
    fresh = qkv_pieces[chained:]
    fresh = [out_part, *fresh] if chained == 0 else fresh
    summing = by_bits(jnp.concatenate(fresh, axis=1))
    for step in range(chip_steps()):
        while chains and chains[-1][0] == step:
            summing = jnp.concatenate([chains.pop()[1], summing], axis=-1)
        summing = halve(summing, "dp", step + 1, chip_steps() - 1 - step)
        if step == 0:
            summing = after(summing, most_grad)
    summing = jnp.concatenate([value for _, value in chains] + [summing], axis=-1)
    out_sum = summing[:, : mp * width]
    qkv_sum = summing[:, mp * width :].reshape(-1, pairs, 3, PAIR)
    out_sum = over_mp_relative([out_sum[:, j * width : (j + 1) * width] for j in range(mp)])
    qkv_sum = qkv_sum.transpose(2, 0, 1, 3).reshape(3, -1, width)

    head_biases = lax.dynamic_update_slice_in_dim(
        jnp.zeros((2, width * mp), jnp.float32),
        jnp.concatenate(bias_pieces, axis=1),
        column_start,
        1,
    )
    for name in ("mp", "dp"):
        bits = bits_of(lax.axis_size(name))
        for first in range(0, bits, 2):
            masks = [mask << first for mask in range(1, 1 << min(2, bits - first))]
            got = [swap(head_biases, name, mask) for mask in masks]
            head_biases = head_biases + got[0]
            head_biases = head_biases + (got[1] + got[2]) if len(got) == 3 else head_biases
    bias_sum = jnp.concatenate([head_biases, late_biases], axis=0)

    grad_scale = lax.rsqrt(jnp.float32(tokens * dp))
    step_value = jnp.float32(ADAM_STEP)
    new_qkv, next_qkv = adam_update(qkv_weight, qkv_moments, qkv_sum * grad_scale, step_value)
    new_out, next_out = adam_update(out_weight, out_moments, out_sum * grad_scale, step_value)
    new_up, next_up = adam_update(up_weight, up_moments, up_sum * grad_scale, step_value)
    new_down, next_down = adam_update(down_weight, down_moments, down_sum * grad_scale, step_value)
    new_gains, next_gains = adam_update(norm_gains, gain_moments, gain_sum * grad_scale, step_value)
    new_biases, next_biases = adam_update(
        bias_rows, bias_moments, bias_sum * grad_scale, step_value
    )
    new_up_bias, next_up_bias = adam_update(
        up_bias, up_bias_moments, unit_sum * grad_scale, step_value
    )
    factor = jnp.sqrt(clip_tau / jnp.maximum(local_max, clip_tau))
    column = jnp.repeat(factor, HEAD_DIM)
    scales = jnp.stack([column, column, jnp.ones_like(column)])[:, None, :]
    new_qkv = new_qkv * scales
    return (
        result.astype(jnp.bfloat16),
        input_grad,
        new_qkv,
        new_out,
        new_up,
        new_down,
        new_gains,
        new_biases,
        new_up_bias,
        next_qkv,
        next_out,
        next_up,
        next_down,
        next_gains,
        next_biases,
        next_up_bias,
    )


def solution(mesh):
    placed = (
        P("dp", None),
        P(("dp", "mp"), None),
        P("dp", None),
        P(None, "dp", "mp"),
        P("dp", "mp"),
        P("dp", "mp"),
        P("dp", "mp"),
        P(),
        P(),
        P(),
        P(None, None, "dp", "mp"),
        P(None, "dp", "mp"),
        P(None, "dp", "mp"),
        P(None, "dp", "mp"),
        P(),
        P(),
        P(),
    )
    return jax.shard_map(
        body,
        mesh=mesh,
        in_specs=placed,
        out_specs=(
            P(("dp", "mp"), None),
            P(("dp", "mp"), None),
            P(None, "dp", "mp"),
            P("dp", "mp"),
            P("dp", "mp"),
            P("dp", "mp"),
            P(),
            P(),
            P(),
            P(None, None, "dp", "mp"),
            P(None, "dp", "mp"),
            P(None, "dp", "mp"),
            P(None, "dp", "mp"),
            P(),
            P(),
            P(),
        ),
        check_vma=False,
    )
```
